512 devices in a mesh: dp: 128 (over y, z, core), sub: 4 (over x).
Axes of the slice: x: 4, y: 8, z: 8, core: 2. Of those that a mesh axis runs over, the one named last changes fastest.
Arguments:
- tokens: bfloat16 [256, 7168], P('dp', 'sub'), may hold values from -10.5 to 10.5
- new_tokens: int32 [128], P('dp'), may hold values from 1 to 2, as said below
- dense_gain: float32 [7168], P('sub'), may hold values from 0.25 to 1.75
- dense_gate: bfloat16 [7168, 18432], P('sub', 'dp'), may hold values from -0.0625 to 0.0625
- dense_up: bfloat16 [7168, 18432], P('sub', 'dp'), may hold values from -0.0625 to 0.0625
- dense_down: bfloat16 [18432, 7168], P('dp', 'sub'), may hold values from -0.046875 to 0.046875
- moe_gain: float32 [7168], P('sub'), may hold values from 0.25 to 1.75
- expert_ids: int32 [256, 8], P('dp'), may hold values from 0 to 15, all different within a row; in each aligned block of 2 rows (0 to 1, 2 to 3, ...) at most 2 rows name the same one
- expert_weights: float32 [256, 8], P('dp'), may hold values from 0.1 to 1
- expert_gate: bfloat16 [7168, 32768], P('sub', 'dp'), may hold values from -0.0625 to 0.0625
- expert_up: bfloat16 [7168, 32768], P('sub', 'dp'), may hold values from -0.0625 to 0.0625
- expert_down: bfloat16 [32768, 7168], P('dp', 'sub'), may hold values from -0.125 to 0.125
Outputs:
- result: bfloat16 [256, 7168], P('dp', 'sub')
The draws below stay inside these ranges and needn't reach their ends.
Inputs may be any that keep to these rules, and one draw needn't show every extreme that they name: `new_tokens`: some request group is full in every draw. `expert_ids`: each row names 8 different experts. Among the 2 rows of one request group no expert is named by more than 2 rows, and in every draw some expert is named by exactly 2 rows of some group.
All inputs are finite; a program needn't handle non-finite values.
Results may differ from the reference program's by a relative error of at most 0.022.
Values may be sent and summed in bfloat16 or wider, within the bound.
A program may use at most 64 MiB of HBM per device.

```python
import math
import jax
import jax.numpy as jnp
import numpy as np
from jax import lax

D = 7168
FF = 18432
EH = 2048
EXPERTS = 16
TOP = 8
ROWS = 2
CAP = 2
GROUPS = 128
TOKENS = 256


def draw_tokens(key, part):
    key = jax.random.fold_in(key, 7)
    position = jnp.arange(D, dtype=jnp.float32) / (D - 1)
    column_scale = 0.3 * jnp.exp(position * jnp.log(10.0))
    values = jnp.clip(jax.random.normal(key, (TOKENS, D), jnp.float32), -3.5, 3.5)
    return (values * column_scale[None, :]).astype(jnp.bfloat16)


def draw_new_tokens(key, part):
    key = jax.random.fold_in(key, 1)
    first_key, second = jax.random.split(key)
    counts = jax.random.randint(first_key, (GROUPS,), 1, ROWS + 1)
    filled = jax.random.randint(second, (), 0, GROUPS)
    return jnp.where(jnp.arange(GROUPS) == filled, ROWS, counts).astype(jnp.int32)


def steps_of(own_key, shape, pieces, low, top_value):
    gain = 1.0
    for dim, blocks in pieces:
        steps = jax.random.uniform(jax.random.fold_in(jax.random.fold_in(own_key, 6), dim), (blocks,), jnp.float32, low / len(pieces), top_value / len(pieces))
        gain = gain * jnp.repeat(jnp.exp(steps), shape[dim] // blocks).reshape((-1,) + (1,) * (len(shape) - 1 - dim))
    return gain


def assign_block(key, own, number, rows, number_of, top, bound, skew):
    ranking = jax.random.permutation(key, number_of)
    heavy_load, common = shares(number_of, rows * top, bound, skew, True), shares(number_of, rows * top, bound, skew, False)
    places = jnp.arange(number_of)

    def named(tallies, rotation):
        used = int((tallies > 0).sum())
        fixed = max(1, used // 4)
        passed = fixed + (places - fixed + rotation * (used - fixed)) % max(1, number_of - fixed)
        return jnp.zeros((number_of,), jnp.int32).at[ranking[jnp.where(places < fixed, places, passed)]].set(jnp.asarray(tallies, jnp.int32))

    tallies = jnp.where(number % 4 == 0, named(heavy_load, number // 4), named(common, number - number // 4 - 1))
    mixed = jax.random.permutation(jax.random.fold_in(own, 3), number_of)
    giver, taker = mixed[0:number_of // 2 * 2:2], mixed[1:number_of // 2 * 2:2]
    room = jnp.minimum(tallies[giver] - 1, bound - tallies[taker]) // 2
    room = jnp.where((giver == ranking[0]) | (taker == ranking[0]) | (tallies[taker] == 0), 0, jnp.maximum(room, 0))
    passed = jax.random.randint(jax.random.fold_in(own, 4), (number_of // 2,), 0, 1 << 20) % (room + 1)
    tallies = tallies.at[giver].add(-passed).at[taker].add(passed)
    items = jnp.searchsorted(jnp.cumsum(tallies), jnp.arange(rows * top), side="right").astype(jnp.int32)
    table = items.reshape(top, rows).T
    table = table[jax.random.permutation(jax.random.fold_in(own, 1), rows)]
    rotation = jax.random.randint(jax.random.fold_in(own, 2), (rows, 1), 0, top)
    return jnp.take_along_axis(table, (jnp.arange(top)[None, :] + rotation) % top, axis=1)


def shares(amount, total, reach, lean, full):
    portions = [(1 << 20) // math.isqrt(rank ** lean) + 1 for rank in range(1, amount + 1)]
    largest = reach if full else min(reach, max(-(-total // amount), total * portions[0] // sum(portions)))
    least = 1 if total - largest >= amount - 1 else 0
    given, spare = [largest] + [least] * (amount - 1), total - largest - least * (amount - 1)
    while spare > 0:
        free = [i for i in range(1, amount) if given[i] < largest] or [i for i in range(1, amount) if given[i] < reach]
        whole, budget = sum([portions[i] for i in free]), spare
        for i in free:
            addition = min(reach - given[i], max(1, budget * portions[i] // whole), spare)
            given[i] = given[i] + addition
            spare = spare - addition
    return np.array(given)


def noise(key, extent, deviation, limit, shards=(), kind=jnp.bfloat16):
    loudness = steps_of(key, extent, shards, -0.22, 0.18) if shards else 1.0
    entries = jax.random.normal(key, extent, jnp.float32) * deviation * loudness
    return jnp.minimum(jnp.maximum(entries, -limit), limit).astype(kind)


def setup_inputs(seed: int = 0) -> dict:
    seeds = jax.random.split(jax.random.key(seed), 13)
    tokens = draw_tokens(jax.random.fold_in(seeds[12], 71), 0)
    new_tokens = draw_new_tokens(jax.random.fold_in(seeds[12], 71), 0)
    dense_gain = jnp.clip(1.0 + 0.15 * jax.random.normal(seeds[2], (D,), jnp.float32), 0.25, 1.75)
    dense_gate = noise(seeds[3], (D, FF), D ** -0.5, 0.0625, ((0, 4), (1, 128)))
    dense_up = noise(seeds[4], (D, FF), D ** -0.5, 0.0625, ((0, 4), (1, 128)))
    dense_down = noise(seeds[5], (FF, D), FF ** -0.5, 0.046875, ((0, 128), (1, 4)))
    moe_gain = jnp.clip(1.0 + 0.15 * jax.random.normal(seeds[6], (D,), jnp.float32), 0.25, 1.75)
    expert_ids_keys = jax.random.split(jax.random.fold_in(seeds[7], 1), TOKENS // ROWS)
    expert_ids_turns = jax.random.permutation(jax.random.fold_in(seeds[7], 3), TOKENS // ROWS)
    expert_ids = jax.vmap(lambda own, number: assign_block(jax.random.fold_in(seeds[7], 2), own, number, ROWS, EXPERTS, TOP, CAP, 1))(expert_ids_keys, expert_ids_turns).reshape((TOKENS, TOP))
    expert_weights = jnp.clip(jnp.exp(math.log(1.0) - 2.3025851 * jax.random.uniform(seeds[8], (TOKENS, TOP), jnp.float32) ** steps_of(seeds[8], (TOKENS, TOP), ((0, 128),), -0.2, 0.2)), 0.1, 1.0)
    expert_gate = noise(seeds[9], (D, EXPERTS * EH), D ** -0.5, 0.0625, ((0, 4), (1, 128)))
    expert_up = noise(seeds[10], (D, EXPERTS * EH), D ** -0.5, 0.0625, ((0, 4), (1, 128)))
    expert_down = noise(seeds[11], (EXPERTS * EH, D), EH ** -0.5, 0.125, ((0, 128), (1, 4)))
    return dict(tokens=tokens, new_tokens=new_tokens, dense_gain=dense_gain, dense_gate=dense_gate, dense_up=dense_up, dense_down=dense_down, moe_gain=moe_gain, expert_ids=expert_ids, expert_weights=expert_weights, expert_gate=expert_gate, expert_up=expert_up, expert_down=expert_down)


def rms_normed(stream, gain_vector):
    widened = stream.astype(jnp.float32)
    scale_factor = lax.rsqrt(lax.optimization_barrier(jnp.mean(widened * widened, axis=1, keepdims=True)) + 1e-06)
    return (widened * scale_factor * gain_vector[None, :]).astype(jnp.bfloat16)

def reference(tokens, new_tokens, dense_gain, dense_gate, dense_up, dense_down, moe_gain, expert_ids, expert_weights, expert_gate, expert_up, expert_down):
    dense_normed = rms_normed(tokens, dense_gain)
    gate_proj = jnp.dot(dense_normed, dense_gate, preferred_element_type=jnp.float32)
    up_proj = jnp.dot(dense_normed, dense_up, preferred_element_type=jnp.float32)
    dense_hidden = (jax.nn.silu(gate_proj) * up_proj).astype(jnp.bfloat16)
    mixed_stream = (tokens.astype(jnp.float32) + jnp.dot(dense_hidden, dense_down, preferred_element_type=jnp.float32)).astype(jnp.bfloat16)
    moe_normed = rms_normed(mixed_stream, moe_gain)
    labels = jnp.arange(EXPERTS, dtype=jnp.int32)
    combine = lax.optimization_barrier(jnp.sum(expert_weights[:, :, None] * (expert_ids[:, :, None] == labels[None, None, :]).astype(jnp.float32), axis=1))

    def one_expert(running_total, expert_index):
        column_start = (expert_index * EH).astype(jnp.int32)
        gate_cols = lax.dynamic_slice_in_dim(expert_gate, column_start, EH, 1)
        up_cols = lax.dynamic_slice_in_dim(expert_up, column_start, EH, 1)
        down_rows = lax.dynamic_slice_in_dim(expert_down, column_start, EH, 0)
        expert_gate_proj = jnp.dot(moe_normed, gate_cols, preferred_element_type=jnp.float32)
        expert_up_proj = jnp.dot(moe_normed, up_cols, preferred_element_type=jnp.float32)
        expert_hidden = (jax.nn.silu(expert_gate_proj) * expert_up_proj).astype(jnp.bfloat16)
        expert_output = jnp.dot(expert_hidden, down_rows, preferred_element_type=jnp.float32)
        mix_weight = lax.dynamic_slice_in_dim(combine, expert_index, 1, 1)
        return (running_total + mix_weight * expert_output, None)
    running_total, _ = lax.scan(one_expert, mixed_stream.astype(jnp.float32), jnp.arange(EXPERTS, dtype=jnp.int32))
    slot_index = jnp.arange(TOKENS, dtype=jnp.int32)
    live_slots = slot_index % ROWS < new_tokens[slot_index // ROWS]
    return jnp.where(live_slots[:, None], running_total, 0.0).astype(jnp.bfloat16)
```

```python
import functools

import jax
import jax.numpy as jnp
from jax import lax
from jax.experimental import pallas as pl
from jax.experimental.pallas import tpu as pltpu
from jax.sharding import PartitionSpec as P

D = 7168
EH = 2048
EXPERTS = 16
TOP = 8
N = 8
NX = 4
DL = 1792
KC = 256
CHUNKS = DL // KC
HALF = 128
XR = HALF // NX
MESH = pl.DeviceIdType.MESH
F32 = jnp.float32
BF16 = jnp.bfloat16
FAR = (4, 3, 5, 2, 6, 1, 7)
NEAR = (1, 7, 2, 6, 3, 5, 4)


def iota(shape, dim):
    return lax.broadcasted_iota(jnp.int32, shape, dim)


def rounded(value):
    return value.astype(BF16).astype(F32)


def kernel(
    tok,
    newt,
    gain1,
    gate,
    up,
    down,
    gain2,
    ids,
    wts,
    egate,
    eup,
    edown,
    out,
    gv,
    uv,
    w1,
    w2,
    w3,
    w4,
    tb,
    gb,
    ab,
    perm,
    gath,
    xm,
    cw,
    px0,
    px1,
    rx0,
    rx1,
    hid,
    cs,
    cr,
    of,
    s1,
    r1,
    s2,
    r2,
    wsem,
    ag1_s,
    ag1_r,
    ag2_s,
    ag2_r,
    fw_s,
    fw_r,
    rx_s,
    rx_r,
    hx_s,
    hx_r,
    co_s,
    co_r,
    r1_s,
    r1_r,
    r2_s,
    r2_r,
):
    dp = lax.axis_index("dp")
    x = lax.axis_index("sub")
    c = lax.rem(dp, 2)
    y = dp // (2 * N)
    z = lax.rem(dp // 2, N)
    a1 = y * (1 - c) + z * c
    a2 = z * (1 - c) + y * c

    def place(i1, i2):
        return (((i1 * N + i2) * (1 - c) + (i2 * N + i1) * c) * 2 + c, x)

    def peer1(d):
        return place(lax.rem(a1 + d, N), a2)

    def peer2(d):
        return place(a1, lax.rem(a2 + d, N))

    def peerx(d):
        return (dp, lax.rem(x + d, NX))

    sibling = (dp + 1 - 2 * c, x)

    def send(src, dst, ssem, rsem, device):
        return pltpu.make_async_remote_copy(
            src_ref=src,
            dst_ref=dst,
            send_sem=ssem,
            recv_sem=rsem,
            device_id=device,
            device_id_type=MESH,
        )

    barrier = pltpu.get_barrier_semaphore()
    for d in range(1, N):
        pl.semaphore_signal(barrier, inc=1, device_id=peer2(d), device_id_type=MESH)
        pl.semaphore_signal(barrier, inc=1, device_id=peer1(d), device_id_type=MESH)
    for d in range(1, NX):
        pl.semaphore_signal(barrier, inc=1, device_id=peerx(d), device_id_type=MESH)
    pl.semaphore_signal(barrier, inc=1, device_id=sibling, device_id_type=MESH)

    loads = [
        pltpu.make_async_copy(src, dst, wsem.at[i])
        for i, (src, dst) in enumerate(
            (
                (gate, gv),
                (up, uv),
                (gate.at[:, pl.ds(0, 128)], w1.at[pl.ds(0, DL), pl.ds(0, 128)]),
                (up.at[:, pl.ds(0, 128)], w1.at[pl.ds(0, DL), pl.ds(128, 128)]),
                (down, w2.at[pl.ds(0, 144), :]),
                (egate, w3.at[pl.ds(0, DL), pl.ds(0, 256)]),
                (eup, w3.at[pl.ds(0, DL), pl.ds(256, 256)]),
                (edown, w4),
            )
        )
    ]
    for load in loads:
        load.start()

    row = iota((16, KC), 0)
    lane = iota((16, KC), 1)
    odd = lax.rem(row, 2) == 1

    def sums_of_squares(block):
        each = jnp.sum(block * block, axis=1, keepdims=True)
        each = jnp.broadcast_to(each, (16, KC))
        even_sum = jnp.sum(jnp.where(odd, 0.0, each), axis=0, keepdims=True)
        odd_sum = jnp.sum(jnp.where(odd, each, 0.0), axis=0, keepdims=True)
        total = jnp.where(odd, odd_sum, even_sum)
        high = rounded(total)
        middle = rounded(total - high)
        low = total - high - middle
        return jnp.where(
            lane == 32, high, jnp.where(lane == 33, middle, jnp.where(lane == 34, low, 0.0))
        )

    def fill_gain(gain):
        gb[...] = jnp.zeros((16, KC), F32)
        for k in range(CHUNKS):
            gb[2 * k : 2 * k + 2, :] = jnp.broadcast_to(gain[:, KC * k : KC * k + KC], (2, KC))

    stream = tok[...].astype(F32)
    tb[...] = jnp.zeros((16, KC), F32)
    for k in range(CHUNKS):
        tb[2 * k : 2 * k + 2, :] = stream[:, KC * k : KC * k + KC]
    fill_gain(gain1)
    lane2 = iota((2, KC), 1)
    combine = jnp.zeros((2, KC), F32)
    chosen = ids[...]
    weights = wts[...]
    for k in range(TOP):
        combine += jnp.where(chosen[:, k : k + 1] == lax.rem(lane2, EXPERTS), weights[:, k : k + 1], 0.0)
    high = rounded(combine)
    ab[...] = jnp.zeros((16, KC), F32)
    ab[14:16, :] = jnp.where(
        lane2 < EXPERTS, high, jnp.where(lane2 < 2 * EXPERTS, combine - high, 0.0)
    )

    def gather(layer, block, side):
        own_group = c * N + a1
        mine = gath.at[layer, own_group, pl.ds(pl.multiple_of(a2 * 16, 16), 16), :]
        gath[layer, own_group, pl.ds(pl.multiple_of(a2 * 16, 16), 16), :] = jnp.where(
            row < 2 * CHUNKS, block * gb[...], side
        ).astype(BF16)
        if layer == 0:
            pl.semaphore_wait(barrier, 2 * (N - 1) + NX)
        first = [
            send(mine, mine, ag1_s.at[layer, d], ag1_r.at[layer, d], peer2(d)) for d in FAR
        ]
        for copy in first:
            copy.start()
        return first

    def permuted(layer, group):
        moved = jnp.dot(perm[...], gath[layer, group], preferred_element_type=F32).astype(BF16)
        rows = pl.ds(pl.multiple_of(group * 16, 16), 16)
        for k in range(CHUNKS + 1):
            xm[rows, KC * k : KC * k + KC] = moved[16 * k : 16 * k + 16, :]

    def spread(layer, first):
        own_group = c * N + a1
        pending = list(first)
        for copy in first:
            copy.wait_recv()
        line = gath.at[layer, own_group]
        second = {
            d: send(line, line, ag2_s.at[layer, d], ag2_r.at[layer, d], peer1(d)) for d in FAR
        }
        for d in FAR:
            second[d].start()
        pending += second.values()

        def forward(d):
            group = c * N + lax.rem(a1 + N - d, N)
            ref = gath.at[layer, group]
            copy = send(ref, ref, fw_s.at[layer, d], fw_r.at[layer, d], sibling)
            copy.start()
            permuted(layer, group)
            return copy

        forwards = {0: forward(0)}
        for d in NEAR:
            second[d].wait_recv()
            forwards[d] = forward(d)
        pending += forwards.values()
        return pending, forwards

    def rest(layer, forwards):
        for d in (0,) + NEAR:
            forwards[d].wait_recv()
            permuted(layer, (1 - c) * N + lax.rem(a2 + N - d, N))

    halves = (c, 1 - c)

    def half_rows(h):
        return pl.ds(pl.multiple_of(halves[h] * HALF, HALF), HALF)

    def part_rows(h, index):
        return pl.ds(pl.multiple_of(halves[h] * HALF + index * XR, XR), XR)

    def project(layer, h, px, rx, weight):
        px[half_rows(h), :] = jnp.dot(
            xm[half_rows(h), :], weight[...], preferred_element_type=F32
        ).astype(BF16)
        copies = [
            send(
                px.at[part_rows(h, lax.rem(x + d, NX)), :],
                rx.at[h, d],
                rx_s.at[layer, h, d],
                rx_r.at[layer, h, d],
                peerx(d),
            )
            for d in (2, 1, 3)
        ]
        for copy in copies:
            copy.start()
        return copies

    def activate(layer, h, px, rx, copies):
        total = px[part_rows(h, x), :].astype(F32)
        for copy, d in zip(copies, (2, 1, 3)):
            copy.wait_recv()
            total = total + rx[h, d].astype(F32)
        tail = total[:, total.shape[1] - 128 :]
        spot = iota((XR, 128), 1)
        if layer == 0:
            used = (spot >= 96) & (spot < 99)
        else:
            used = spot < 3
        squares = jnp.sum(jnp.where(used, tail, 0.0), axis=1, keepdims=True)
        scale = lax.rsqrt(squares / D + 1e-06)
        if layer == 0:
            main = jax.nn.silu(total[:, :128] * scale) * (total[:, 128:256] * scale)
            last = jax.nn.silu(tail * scale) * (pltpu.roll(tail, 64, 1) * scale)
            last = jnp.where(spot < 16, last, 0.0)
            value = jnp.concatenate((main, last), axis=1)
        else:
            value = jax.nn.silu(total[:, :256] * scale) * (total[:, 256:512] * scale)
            share = cw[part_rows(h, x), :]
            value = value * jnp.concatenate((share, share), axis=1)
        rows = part_rows(h, x)
        hid[layer, rows, :] = value.astype(BF16)
        mine = hid.at[layer, rows, :]
        out_copies = [
            send(mine, mine, hx_s.at[layer, h, d], hx_r.at[layer, h, d], peerx(d)) for d in (2, 1, 3)
        ]
        for copy in out_copies:
            copy.start()
        return out_copies

    def lower(layer, weight, hx):
        for copy in hx[0]:
            copy.wait_recv()
        value = hid[layer, half_rows(0), :]
        for k in range(CHUNKS):
            of[:, KC * k : KC * k + KC] = jnp.dot(
                value, weight[:, KC * k : KC * k + KC], preferred_element_type=F32
            )
        for copy in hx[1]:
            copy.wait_recv()
        value = hid[layer, half_rows(1), :]
        for k in range(CHUNKS):
            cs[layer, :, KC * k : KC * k + KC] = jnp.dot(
                value, weight[:, KC * k : KC * k + KC], preferred_element_type=F32
            ).astype(BF16)

    def chunk_rows(index):
        return pl.ds(pl.multiple_of(index * 16, 16), 16)

    def scatter(layer):
        cross = {}
        for d in FAR + (0,):
            rows = chunk_rows(lax.rem(a2 + d, N))
            cross[d] = send(
                cs.at[layer, rows, :],
                cr.at[layer, rows, :],
                co_s.at[layer, d],
                co_r.at[layer, d],
                sibling,
            )
            cross[d].start()
        pending = list(cross.values())
        first = {}
        for d in FAR + (0,):
            rows = chunk_rows(lax.rem(a1 + d, N))
            cross[d].wait_recv()
            value = of[rows, :] + cr[layer, rows, :].astype(F32)
            if d:
                s1[layer, rows, :] = value.astype(BF16)
                first[d] = send(
                    s1.at[layer, rows, :],
                    r1.at[layer, d],
                    r1_s.at[layer, d],
                    r1_r.at[layer, d],
                    peer1(d),
                )
                first[d].start()
        total = value
        for d in NEAR:
            first[d].wait_recv()
            total = total + r1[layer, d].astype(F32)
        pending += first.values()
        total = total.astype(BF16)
        stacked = jnp.concatenate(
            [total[:, KC * k : KC * k + KC] for k in range(CHUNKS)] + [jnp.zeros((16, KC), BF16)],
            axis=0,
        )
        s2[layer] = jnp.dot(perm[...], stacked, preferred_element_type=F32).astype(BF16)
        second = {}
        for d in FAR:
            second[d] = send(
                s2.at[layer, chunk_rows(lax.rem(a2 + d, N)), :],
                r2.at[layer, d],
                r2_s.at[layer, d],
                r2_r.at[layer, d],
                peer2(d),
            )
            second[d].start()
        total = s2[layer, chunk_rows(a2), :].astype(F32)
        for d in NEAR:
            second[d].wait_recv()
            total = total + r2[layer, d].astype(F32)
        pending += second.values()
        return total, pending

    def layer_of(layer, block, side, px, rx, w_in, w_out, prepare, loads_in, loads_out):
        first = gather(layer, block, side)
        prepare()
        pending, forwards = spread(layer, first)
        for load in loads_in:
            load.wait()
        if layer == 0:
            cw[half_rows(0), :] = jnp.dot(
                xm[half_rows(0), DL:], selector, preferred_element_type=F32
            )
        x0 = project(layer, 0, px, rx, w_in)
        rest(layer, forwards)
        x1 = project(layer, 1, px, rx, w_in)
        if layer == 0:
            cw[half_rows(1), :] = jnp.dot(
                xm[half_rows(1), DL:], selector, preferred_element_type=F32
            )
        h0 = activate(layer, 0, px, rx, x0)
        h1 = activate(layer, 1, px, rx, x1)
        for load in loads_out:
            load.wait()
        lower(layer, w_out, (h0, h1))
        total, more = scatter(layer)
        return total, pending + x0 + x1 + h0 + h1 + more

    expert = dp // (EH // 256)
    at = iota((KC, 128), 0)
    selector = ((at == expert) | (at == expert + EXPERTS)).astype(F32).astype(BF16)

    def prepare():
        to = iota((128, 128), 0)
        source = lax.rem(to // 2, 8) * 16 + (to // 16) * 2 + lax.rem(to, 2)
        perm[...] = (source == iota((128, 128), 1)).astype(F32).astype(BF16)
        side_row = iota((KC, 128), 0)
        side_lane = iota((KC, 128), 1)
        is_part = (side_row >= 32) & (side_row < 35)
        w1[DL:, :256] = jnp.zeros((KC, 256), BF16)
        w1[DL:, 256:] = (is_part & (side_lane == side_row + 64)).astype(F32).astype(BF16)
        w2[144:, :] = jnp.zeros((112, DL), BF16)
        w3[DL:, :512] = jnp.zeros((KC, 512), BF16)
        w3[:DL, 512:] = jnp.zeros((DL, 128), BF16)
        w3[DL:, 512:] = (is_part & (side_lane == side_row - 32)).astype(F32).astype(BF16)
        loads[0].wait()
        loads[1].wait()

        def tails(i, carry):
            rows = pl.ds(pl.multiple_of(i * KC, KC), KC)
            blank = jnp.zeros((KC, 48), BF16)
            w1[rows, 256:] = jnp.concatenate((gv[rows, 128:], blank, uv[rows, 128:], blank), axis=1)
            return carry

        lax.fori_loop(0, CHUNKS, tails, 0)

    tokens_block = tb[...]
    side = jnp.where(row >= 14, ab[...] + sums_of_squares(tokens_block), 0.0)
    dense, pending = layer_of(
        0, tokens_block, side, px0, rx0, w1, w2, prepare, loads[2:4], loads[4:5]
    )
    fill_gain(gain2)
    mixed = rounded(tb[...] + dense)
    mixed = jnp.where(row < 2 * CHUNKS, mixed, 0.0)
    tb[...] = mixed
    side = jnp.where(row >= 14, sums_of_squares(mixed), 0.0)
    routed, more = layer_of(
        1, mixed, side, px1, rx1, w3, w4, lambda: None, loads[5:7], loads[7:]
    )
    tb[...] = tb[...] + routed
    live = iota((2, KC), 0) < newt[0]
    for k in range(CHUNKS):
        out[:, KC * k : KC * k + KC] = jnp.where(live, tb[2 * k : 2 * k + 2, :], 0.0)
    for copy in pending + more:
        copy.wait_send()


def shards(
    tokens,
    new_tokens,
    dense_gain,
    dense_gate,
    dense_up,
    dense_down,
    moe_gain,
    expert_ids,
    expert_weights,
    expert_gate,
    expert_up,
    expert_down,
):
    vmem = pl.BlockSpec(memory_space=pltpu.VMEM)
    smem = pl.BlockSpec(memory_space=pltpu.SMEM)
    anywhere = pl.BlockSpec(memory_space=pl.ANY)
    sems = pltpu.SemaphoreType.DMA
    result = pl.pallas_call(
        kernel,
        out_shape=jax.ShapeDtypeStruct((2, DL), F32),
        in_specs=[
            vmem,
            smem,
            vmem,
            anywhere,
            anywhere,
            anywhere,
            vmem,
            vmem,
            vmem,
            anywhere,
            anywhere,
            anywhere,
        ],
        out_specs=vmem,
        scratch_shapes=[
            pltpu.VMEM((DL, 144), BF16),
            pltpu.VMEM((DL, 144), BF16),
            pltpu.VMEM((DL + KC, 384), BF16),
            pltpu.VMEM((256, DL), BF16),
            pltpu.VMEM((DL + KC, 640), BF16),
            pltpu.VMEM((256, DL), BF16),
            pltpu.VMEM((16, KC), F32),
            pltpu.VMEM((16, KC), F32),
            pltpu.VMEM((16, KC), F32),
            pltpu.VMEM((128, 128), BF16),
            pltpu.VMEM((2, 2 * N, 128, KC), BF16),
            pltpu.VMEM((2 * HALF, DL + KC), BF16),
            pltpu.VMEM((2 * HALF, 128), F32),
            pltpu.VMEM((2 * HALF, 384), BF16),
            pltpu.VMEM((2 * HALF, 640), BF16),
            pltpu.VMEM((2, NX, XR, 384), BF16),
            pltpu.VMEM((2, NX, XR, 640), BF16),
            pltpu.VMEM((2, 2 * HALF, 256), BF16),
            pltpu.VMEM((2, HALF, DL), BF16),
            pltpu.VMEM((2, HALF, DL), BF16),
            pltpu.VMEM((HALF, DL), F32),
            pltpu.VMEM((2, HALF, DL), BF16),
            pltpu.VMEM((2, N, 16, DL), BF16),
            pltpu.VMEM((2, 128, KC), BF16),
            pltpu.VMEM((2, N, 16, KC), BF16),
            sems((8,)),
            sems((2, N)),
            sems((2, N)),
            sems((2, N)),
            sems((2, N)),
            sems((2, N)),
            sems((2, N)),
            sems((2, 2, NX)),
            sems((2, 2, NX)),
            sems((2, 2, NX)),
            sems((2, 2, NX)),
            sems((2, N)),
            sems((2, N)),
            sems((2, N)),
            sems((2, N)),
            sems((2, N)),
            sems((2, N)),
        ],
        compiler_params=pltpu.CompilerParams(
            collective_id=0, has_side_effects=True, vmem_limit_bytes=48 * 1024 * 1024
        ),
        name="layers",
    )(
        tokens,
        new_tokens,
        dense_gain.reshape(1, DL),
        dense_gate,
        dense_up,
        dense_down,
        moe_gain.reshape(1, DL),
        expert_ids,
        expert_weights,
        expert_gate,
        expert_up,
        expert_down,
    )
    return result.astype(BF16)


def solution(mesh):
    placed = (
        P("dp", "sub"),
        P("dp"),
        P("sub"),
        P("sub", "dp"),
        P("sub", "dp"),
        P("dp", "sub"),
        P("sub"),
        P("dp", None),
        P("dp", None),
        P("sub", "dp"),
        P("sub", "dp"),
        P("dp", "sub"),
    )
    return jax.shard_map(
        shards, mesh=mesh, in_specs=placed, out_specs=P("dp", "sub"), check_vma=False
    )
```

```python
import functools

import jax
import jax.numpy as jnp
from jax import lax
from jax.experimental import pallas as pl
from jax.experimental.pallas import tpu as pltpu
from jax.sharding import PartitionSpec as P

D = 7168
EH = 2048
EXPERTS = 16
TOP = 8
N = 8
NX = 4
DL = 1792
KC = 256
CHUNKS = DL // KC
HALF = 128
XR = HALF // NX
MESH = pl.DeviceIdType.MESH
F32 = jnp.float32
BF16 = jnp.bfloat16
FAR = (4, 3, 5, 2, 6, 1, 7)
NEAR = (1, 7, 2, 6, 3, 5, 4)


def iota(shape, dim):
    return lax.broadcasted_iota(jnp.int32, shape, dim)


def rounded(value):
    return value.astype(BF16).astype(F32)


def kernel(
    tok,
    newt,
    gain1,
    gate,
    up,
    down,
    gain2,
    ids,
    wts,
    egate,
    eup,
    edown,
    out,
    w1,
    w2,
    w3,
    w4,
    tb,
    gb,
    ab,
    perm,
    gath,
    xm,
    cw,
    px0,
    px1,
    rx0,
    rx1,
    hid,
    cs,
    cr,
    of,
    s1,
    r1,
    s2,
    r2,
    wsem,
    ag1_s,
    ag1_r,
    ag2_s,
    ag2_r,
    fw_s,
    fw_r,
    rx_s,
    rx_r,
    hx_s,
    hx_r,
    co_s,
    co_r,
    r1_s,
    r1_r,
    r2_s,
    r2_r,
):
    dp = lax.axis_index("dp")
    x = lax.axis_index("sub")
    c = lax.rem(dp, 2)
    y = dp // (2 * N)
    z = lax.rem(dp // 2, N)
    a1 = y * (1 - c) + z * c
    a2 = z * (1 - c) + y * c

    def place(i1, i2):
        return (((i1 * N + i2) * (1 - c) + (i2 * N + i1) * c) * 2 + c, x)

    def peer1(d):
        return place(lax.rem(a1 + d, N), a2)

    def peer2(d):
        return place(a1, lax.rem(a2 + d, N))

    def peerx(d):
        return (dp, lax.rem(x + d, NX))

    sibling = (dp + 1 - 2 * c, x)

    def send(src, dst, ssem, rsem, device):
        return pltpu.make_async_remote_copy(
            src_ref=src,
            dst_ref=dst,
            send_sem=ssem,
            recv_sem=rsem,
            device_id=device,
            device_id_type=MESH,
        )

    barrier = pltpu.get_barrier_semaphore()
    for d in range(1, N):
        pl.semaphore_signal(barrier, inc=1, device_id=peer2(d), device_id_type=MESH)
        pl.semaphore_signal(barrier, inc=1, device_id=peer1(d), device_id_type=MESH)
    for d in range(1, NX):
        pl.semaphore_signal(barrier, inc=1, device_id=peerx(d), device_id_type=MESH)
    pl.semaphore_signal(barrier, inc=1, device_id=sibling, device_id_type=MESH)

    loads = [
        pltpu.make_async_copy(src, dst, wsem.at[i])
        for i, (src, dst) in enumerate(
            (
                (gate.at[pl.ds(0, 128), :], w1.at[pl.ds(0, 128), pl.ds(0, DL)]),
                (up.at[pl.ds(0, 128), :], w1.at[pl.ds(128, 128), pl.ds(0, DL)]),
                (gate.at[pl.ds(128, 16), :], w1.at[pl.ds(256, 16), pl.ds(0, DL)]),
                (up.at[pl.ds(128, 16), :], w1.at[pl.ds(320, 16), pl.ds(0, DL)]),
                (down, w2.at[pl.ds(0, 144), :]),
                (egate, w3.at[pl.ds(0, DL), pl.ds(0, 256)]),
                (eup, w3.at[pl.ds(0, DL), pl.ds(256, 256)]),
                (edown, w4),
            )
        )
    ]
    for load in loads:
        load.start()

    row = iota((16, KC), 0)
    lane = iota((16, KC), 1)
    odd = lax.rem(row, 2) == 1

    def sums_of_squares(block):
        each = jnp.sum(block * block, axis=1, keepdims=True)
        each = jnp.broadcast_to(each, (16, KC))
        even_sum = jnp.sum(jnp.where(odd, 0.0, each), axis=0, keepdims=True)
        odd_sum = jnp.sum(jnp.where(odd, each, 0.0), axis=0, keepdims=True)
        total = jnp.where(odd, odd_sum, even_sum)
        high = rounded(total)
        middle = rounded(total - high)
        low = total - high - middle
        return jnp.where(
            lane == 32, high, jnp.where(lane == 33, middle, jnp.where(lane == 34, low, 0.0))
        )

    def fill_gain(gain):
        gb[...] = jnp.zeros((16, KC), F32)
        for k in range(CHUNKS):
            gb[2 * k : 2 * k + 2, :] = jnp.broadcast_to(gain[KC * k : KC * k + KC][None, :], (2, KC))

    stream = tok[...].astype(F32)
    tb[...] = jnp.zeros((16, KC), F32)
    for k in range(CHUNKS):
        tb[2 * k : 2 * k + 2, :] = stream[:, KC * k : KC * k + KC]
    fill_gain(gain1)
    lane2 = iota((2, KC), 1)
    combine = jnp.zeros((2, KC), F32)
    chosen = ids[...]
    weights = wts[...]
    for k in range(TOP):
        combine += jnp.where(chosen[:, k : k + 1] == lax.rem(lane2, EXPERTS), weights[:, k : k + 1], 0.0)
    high = rounded(combine)
    ab[...] = jnp.zeros((16, KC), F32)
    ab[14:16, :] = jnp.where(
        lane2 < EXPERTS, high, jnp.where(lane2 < 2 * EXPERTS, combine - high, 0.0)
    )

    def gather(layer, block, side):
        own_group = c * N + a1
        mine = gath.at[layer, own_group, pl.ds(pl.multiple_of(a2 * 16, 16), 16), :]
        gath[layer, own_group, pl.ds(pl.multiple_of(a2 * 16, 16), 16), :] = jnp.where(
            row < 2 * CHUNKS, block * gb[...], side
        ).astype(BF16)
        if layer == 0:
            pl.semaphore_wait(barrier, 2 * (N - 1) + NX)
        first = [
            send(mine, mine, ag1_s.at[layer, d], ag1_r.at[layer, d], peer2(d)) for d in FAR
        ]
        for copy in first:
            copy.start()
        return first

    def permuted(layer, group):
        moved = jnp.dot(perm[...], gath[layer, group], preferred_element_type=F32).astype(BF16)
        rows = pl.ds(pl.multiple_of(group * 16, 16), 16)
        for k in range(CHUNKS + 1):
            xm[rows, KC * k : KC * k + KC] = moved[16 * k : 16 * k + 16, :]

    def spread(layer, first):
        own_group = c * N + a1
        pending = list(first)
        for copy in first:
            copy.wait_recv()
        line = gath.at[layer, own_group]
        second = {
            d: send(line, line, ag2_s.at[layer, d], ag2_r.at[layer, d], peer1(d)) for d in FAR
        }
        for d in FAR:
            second[d].start()
        pending += second.values()

        def forward(d):
            group = c * N + lax.rem(a1 + N - d, N)
            ref = gath.at[layer, group]
            copy = send(ref, ref, fw_s.at[layer, d], fw_r.at[layer, d], sibling)
            copy.start()
            permuted(layer, group)
            return copy

        forwards = {0: forward(0)}
        for d in NEAR:
            second[d].wait_recv()
            forwards[d] = forward(d)
        pending += forwards.values()
        return pending, forwards

    def rest(layer, forwards):
        for d in (0,) + NEAR:
            forwards[d].wait_recv()
            permuted(layer, (1 - c) * N + lax.rem(a2 + N - d, N))

    halves = (c, 1 - c)

    def half_rows(h):
        return pl.ds(pl.multiple_of(halves[h] * HALF, HALF), HALF)

    def part_rows(h, index):
        return pl.ds(pl.multiple_of(halves[h] * HALF + index * XR, XR), XR)

    def project(layer, h, px, rx, weight):
        px[half_rows(h), :] = lax.dot_general(
            xm[half_rows(h), :],
            weight[...],
            (((1,), (1 - layer,)), ((), ())),
            preferred_element_type=F32,
        ).astype(BF16)
        copies = [
            send(
                px.at[part_rows(h, lax.rem(x + d, NX)), :],
                rx.at[h, d],
                rx_s.at[layer, h, d],
                rx_r.at[layer, h, d],
                peerx(d),
            )
            for d in (2, 1, 3)
        ]
        for copy in copies:
            copy.start()
        return copies

    def activate(layer, h, px, rx, copies):
        total = px[part_rows(h, x), :].astype(F32)
        for copy, d in zip(copies, (2, 1, 3)):
            copy.wait_recv()
            total = total + rx[h, d].astype(F32)
        tail = total[:, total.shape[1] - 128 :]
        spot = iota((XR, 128), 1)
        if layer == 0:
            used = (spot >= 96) & (spot < 99)
        else:
            used = spot < 3
        squares = jnp.sum(jnp.where(used, tail, 0.0), axis=1, keepdims=True)
        scale = lax.rsqrt(squares / D + 1e-06)
        if layer == 0:
            main = jax.nn.silu(total[:, :128] * scale) * (total[:, 128:256] * scale)
            last = jax.nn.silu(tail * scale) * (pltpu.roll(tail, 64, 1) * scale)
            last = jnp.where(spot < 16, last, 0.0)
            value = jnp.concatenate((main, last), axis=1)
        else:
            value = jax.nn.silu(total[:, :256] * scale) * (total[:, 256:512] * scale)
            share = cw[part_rows(h, x), :]
            value = value * jnp.concatenate((share, share), axis=1)
        rows = part_rows(h, x)
        hid[layer, rows, :] = value.astype(BF16)
        mine = hid.at[layer, rows, :]
        out_copies = [
            send(mine, mine, hx_s.at[layer, h, d], hx_r.at[layer, h, d], peerx(d)) for d in (2, 1, 3)
        ]
        for copy in out_copies:
            copy.start()
        return out_copies

    def lower(layer, weight, hx):
        for copy in hx[0]:
            copy.wait_recv()
        value = hid[layer, half_rows(0), :]
        for k in range(CHUNKS):
            of[:, KC * k : KC * k + KC] = jnp.dot(
                value, weight[:, KC * k : KC * k + KC], preferred_element_type=F32
            )
        for copy in hx[1]:
            copy.wait_recv()
        value = hid[layer, half_rows(1), :]
        for k in range(CHUNKS):
            cs[layer, :, KC * k : KC * k + KC] = jnp.dot(
                value, weight[:, KC * k : KC * k + KC], preferred_element_type=F32
            ).astype(BF16)

    def chunk_rows(index):
        return pl.ds(pl.multiple_of(index * 16, 16), 16)

    def scatter(layer):
        cross = {}
        for d in FAR + (0,):
            rows = chunk_rows(lax.rem(a2 + d, N))
            cross[d] = send(
                cs.at[layer, rows, :],
                cr.at[layer, rows, :],
                co_s.at[layer, d],
                co_r.at[layer, d],
                sibling,
            )
            cross[d].start()
        pending = list(cross.values())
        first = {}
        for d in FAR + (0,):
            rows = chunk_rows(lax.rem(a1 + d, N))
            cross[d].wait_recv()
            value = of[rows, :] + cr[layer, rows, :].astype(F32)
            if d:
                s1[layer, rows, :] = value.astype(BF16)
                first[d] = send(
                    s1.at[layer, rows, :],
                    r1.at[layer, d],
                    r1_s.at[layer, d],
                    r1_r.at[layer, d],
                    peer1(d),
                )
                first[d].start()
        total = value
        for d in NEAR:
            first[d].wait_recv()
            total = total + r1[layer, d].astype(F32)
        pending += first.values()
        total = total.astype(BF16)
        stacked = jnp.concatenate(
            [total[:, KC * k : KC * k + KC] for k in range(CHUNKS)] + [jnp.zeros((16, KC), BF16)],
            axis=0,
        )
        s2[layer] = jnp.dot(perm[...], stacked, preferred_element_type=F32).astype(BF16)
        second = {}
        for d in FAR:
            second[d] = send(
                s2.at[layer, chunk_rows(lax.rem(a2 + d, N)), :],
                r2.at[layer, d],
                r2_s.at[layer, d],
                r2_r.at[layer, d],
                peer2(d),
            )
            second[d].start()
        total = s2[layer, chunk_rows(a2), :].astype(F32)
        for d in NEAR:
            second[d].wait_recv()
            total = total + r2[layer, d].astype(F32)
        pending += second.values()
        return total, pending

    def layer_of(layer, block, side, px, rx, w_in, w_out, prepare, loads_in, loads_out):
        first = gather(layer, block, side)
        prepare()
        pending, forwards = spread(layer, first)
        for load in loads_in:
            load.wait()
        if layer == 0:
            cw[half_rows(0), :] = jnp.dot(
                xm[half_rows(0), DL:], selector, preferred_element_type=F32
            )
        x0 = project(layer, 0, px, rx, w_in)
        rest(layer, forwards)
        x1 = project(layer, 1, px, rx, w_in)
        if layer == 0:
            cw[half_rows(1), :] = jnp.dot(
                xm[half_rows(1), DL:], selector, preferred_element_type=F32
            )
        h0 = activate(layer, 0, px, rx, x0)
        h1 = activate(layer, 1, px, rx, x1)
        for load in loads_out:
            load.wait()
        lower(layer, w_out, (h0, h1))
        total, more = scatter(layer)
        return total, pending + x0 + x1 + h0 + h1 + more

    expert = dp // (EH // 256)
    at = iota((KC, 128), 0)
    selector = ((at == expert) | (at == expert + EXPERTS)).astype(F32).astype(BF16)

    def prepare():
        to = iota((128, 128), 0)
        source = lax.rem(to // 2, 8) * 16 + (to // 16) * 2 + lax.rem(to, 2)
        perm[...] = (source == iota((128, 128), 1)).astype(F32).astype(BF16)
        side_row = iota((KC, 128), 0)
        side_lane = iota((KC, 128), 1)
        is_part = (side_row >= 32) & (side_row < 35)
        w1[:256, DL:] = jnp.zeros((256, KC), BF16)
        w1[272:320, :DL] = jnp.zeros((48, DL), BF16)
        w1[336:, :DL] = jnp.zeros((48, DL), BF16)
        to_row = iota((128, KC), 0)
        to_lane = iota((128, KC), 1)
        wanted = (to_lane >= 32) & (to_lane < 35) & (to_row == to_lane + 64)
        w1[256:, DL:] = wanted.astype(F32).astype(BF16)
        w2[144:, :] = jnp.zeros((112, DL), BF16)
        w3[DL:, :512] = jnp.zeros((KC, 512), BF16)
        w3[:DL, 512:] = jnp.zeros((DL, 128), BF16)
        w3[DL:, 512:] = (is_part & (side_lane == side_row - 32)).astype(F32).astype(BF16)

    tokens_block = tb[...]
    side = jnp.where(row >= 14, ab[...] + sums_of_squares(tokens_block), 0.0)
    dense, pending = layer_of(
        0, tokens_block, side, px0, rx0, w1, w2, prepare, loads[0:4], loads[4:5]
    )
    fill_gain(gain2)
    mixed = rounded(tb[...] + dense)
    mixed = jnp.where(row < 2 * CHUNKS, mixed, 0.0)
    tb[...] = mixed
    side = jnp.where(row >= 14, sums_of_squares(mixed), 0.0)
    routed, more = layer_of(
        1, mixed, side, px1, rx1, w3, w4, lambda: None, loads[5:7], loads[7:]
    )
    tb[...] = tb[...] + routed
    live = iota((2, KC), 0) < newt[0]
    for k in range(CHUNKS):
        out[:, KC * k : KC * k + KC] = jnp.where(live, tb[2 * k : 2 * k + 2, :], 0.0)
    for copy in pending + more:
        copy.wait_send()


def shards(
    tokens,
    new_tokens,
    dense_gain,
    dense_gate,
    dense_up,
    dense_down,
    moe_gain,
    expert_ids,
    expert_weights,
    expert_gate,
    expert_up,
    expert_down,
):
    vmem = pl.BlockSpec(memory_space=pltpu.VMEM)
    smem = pl.BlockSpec(memory_space=pltpu.SMEM)
    anywhere = pl.BlockSpec(memory_space=pltpu.HBM)
    sems = pltpu.SemaphoreType.DMA
    result = pl.pallas_call(
        kernel,
        out_shape=jax.ShapeDtypeStruct((2, DL), F32),
        in_specs=[
            vmem,
            smem,
            vmem,
            anywhere,
            anywhere,
            anywhere,
            vmem,
            vmem,
            vmem,
            anywhere,
            anywhere,
            anywhere,
        ],
        out_specs=vmem,
        scratch_shapes=[
            pltpu.VMEM((384, DL + KC), BF16),
            pltpu.VMEM((256, DL), BF16),
            pltpu.VMEM((DL + KC, 640), BF16),
            pltpu.VMEM((256, DL), BF16),
            pltpu.VMEM((16, KC), F32),
            pltpu.VMEM((16, KC), F32),
            pltpu.VMEM((16, KC), F32),
            pltpu.VMEM((128, 128), BF16),
            pltpu.VMEM((2, 2 * N, 128, KC), BF16),
            pltpu.VMEM((2 * HALF, DL + KC), BF16),
            pltpu.VMEM((2 * HALF, 128), F32),
            pltpu.VMEM((2 * HALF, 384), BF16),
            pltpu.VMEM((2 * HALF, 640), BF16),
            pltpu.VMEM((2, NX, XR, 384), BF16),
            pltpu.VMEM((2, NX, XR, 640), BF16),
            pltpu.VMEM((2, 2 * HALF, 256), BF16),
            pltpu.VMEM((2, HALF, DL), BF16),
            pltpu.VMEM((2, HALF, DL), BF16),
            pltpu.VMEM((HALF, DL), F32),
            pltpu.VMEM((2, HALF, DL), BF16),
            pltpu.VMEM((2, N, 16, DL), BF16),
            pltpu.VMEM((2, 128, KC), BF16),
            pltpu.VMEM((2, N, 16, KC), BF16),
            sems((8,)),
            sems((2, N)),
            sems((2, N)),
            sems((2, N)),
            sems((2, N)),
            sems((2, N)),
            sems((2, N)),
            sems((2, 2, NX)),
            sems((2, 2, NX)),
            sems((2, 2, NX)),
            sems((2, 2, NX)),
            sems((2, N)),
            sems((2, N)),
            sems((2, N)),
            sems((2, N)),
            sems((2, N)),
            sems((2, N)),
        ],
        compiler_params=pltpu.CompilerParams(
            collective_id=0, has_side_effects=True, vmem_limit_bytes=60 * 1024 * 1024
        ),
        name="layers",
    )(
        tokens,
        new_tokens,
        dense_gain,
        dense_gate.T,
        dense_up.T,
        dense_down,
        moe_gain,
        expert_ids,
        expert_weights,
        expert_gate,
        expert_up,
        expert_down,
    )
    return result.astype(BF16)


def solution(mesh):
    placed = (
        P("dp", "sub"),
        P("dp"),
        P("sub"),
        P("sub", "dp"),
        P("sub", "dp"),
        P("dp", "sub"),
        P("sub"),
        P("dp", None),
        P("dp", None),
        P("sub", "dp"),
        P("sub", "dp"),
        P("dp", "sub"),
    )
    return jax.shard_map(
        shards, mesh=mesh, in_specs=placed, out_specs=P("dp", "sub"), check_vma=False
    )
```

```python
import functools

import jax
import jax.numpy as jnp
from jax import lax
from jax.experimental import pallas as pl
from jax.experimental.pallas import tpu as pltpu
from jax.sharding import PartitionSpec as P

D = 7168
EH = 2048
EXPERTS = 16
TOP = 8
N = 8
NX = 4
DL = 1792
KC = 256
CHUNKS = DL // KC
HALF = 128
XR = HALF // NX
MESH = pl.DeviceIdType.MESH
F32 = jnp.float32
BF16 = jnp.bfloat16
FAR = (4, 3, 5, 2, 6, 1, 7)
NEAR = (1, 7, 2, 6, 3, 5, 4)
BATCHES = ((3, 5, 4, 0), (1, 7, 2, 6))


def iota(shape, dim):
    return lax.broadcasted_iota(jnp.int32, shape, dim)


def rounded(value):
    return value.astype(BF16).astype(F32)


def kernel(
    tok,
    newt,
    gain1,
    gate,
    up,
    down,
    gain2,
    ids,
    wts,
    egate,
    eup,
    edown,
    out,
    w1,
    w2,
    w3,
    w4,
    tb,
    gb,
    ab,
    perm,
    gath,
    xm,
    cw,
    px0,
    px1,
    rx0,
    rx1,
    hid,
    cs,
    cr,
    of,
    s1,
    r1,
    s2,
    r2,
    wsem,
    ag1_s,
    ag1_r,
    ag2_s,
    ag2_r,
    fw_s,
    fw_r,
    rx_s,
    rx_r,
    hx_s,
    hx_r,
    co_s,
    co_r,
    r1_s,
    r1_r,
    r2_s,
    r2_r,
):
    dp = lax.axis_index("dp")
    x = lax.axis_index("sub")
    c = lax.rem(dp, 2)
    y = dp // (2 * N)
    z = lax.rem(dp // 2, N)
    a1 = y * (1 - c) + z * c
    a2 = z * (1 - c) + y * c

    def place(i1, i2):
        return (((i1 * N + i2) * (1 - c) + (i2 * N + i1) * c) * 2 + c, x)

    def peer1(d):
        return place(lax.rem(a1 + d, N), a2)

    def peer2(d):
        return place(a1, lax.rem(a2 + d, N))

    def peerx(d):
        return (dp, lax.rem(x + d, NX))

    sibling = (dp + 1 - 2 * c, x)

    def send(src, dst, ssem, rsem, device):
        return pltpu.make_async_remote_copy(
            src_ref=src,
            dst_ref=dst,
            send_sem=ssem,
            recv_sem=rsem,
            device_id=device,
            device_id_type=MESH,
        )

    barrier = pltpu.get_barrier_semaphore()
    for d in range(1, N):
        pl.semaphore_signal(barrier, inc=1, device_id=peer2(d), device_id_type=MESH)
        pl.semaphore_signal(barrier, inc=1, device_id=peer1(d), device_id_type=MESH)
    for d in range(1, NX):
        pl.semaphore_signal(barrier, inc=1, device_id=peerx(d), device_id_type=MESH)
    pl.semaphore_signal(barrier, inc=1, device_id=sibling, device_id_type=MESH)

    loads = [
        pltpu.make_async_copy(src, dst, wsem.at[i])
        for i, (src, dst) in enumerate(
            (
                (gate.at[pl.ds(0, 128), :], w1.at[pl.ds(0, 128), pl.ds(0, DL)]),
                (up.at[pl.ds(0, 128), :], w1.at[pl.ds(128, 128), pl.ds(0, DL)]),
                (gate.at[pl.ds(128, 16), :], w1.at[pl.ds(256, 16), pl.ds(0, DL)]),
                (up.at[pl.ds(128, 16), :], w1.at[pl.ds(320, 16), pl.ds(0, DL)]),
                (down, w2.at[pl.ds(0, 144), :]),
                (egate, w3.at[pl.ds(0, DL), pl.ds(0, 256)]),
                (eup, w3.at[pl.ds(0, DL), pl.ds(256, 256)]),
                (edown, w4),
            )
        )
    ]
    for load in loads:
        load.start()

    row = iota((16, KC), 0)
    lane = iota((16, KC), 1)
    odd = lax.rem(row, 2) == 1

    def sums_of_squares(block):
        each = jnp.sum(block * block, axis=1, keepdims=True)
        each = jnp.broadcast_to(each, (16, KC))
        even_sum = jnp.sum(jnp.where(odd, 0.0, each), axis=0, keepdims=True)
        odd_sum = jnp.sum(jnp.where(odd, each, 0.0), axis=0, keepdims=True)
        total = jnp.where(odd, odd_sum, even_sum)
        high = rounded(total)
        middle = rounded(total - high)
        low = total - high - middle
        return jnp.where(
            lane == 32, high, jnp.where(lane == 33, middle, jnp.where(lane == 34, low, 0.0))
        )

    def fill_gain(gain):
        gb[...] = jnp.zeros((16, KC), F32)
        for k in range(CHUNKS):
            gb[2 * k : 2 * k + 2, :] = jnp.broadcast_to(gain[KC * k : KC * k + KC][None, :], (2, KC))

    stream = tok[...].astype(F32)
    tb[...] = jnp.zeros((16, KC), F32)
    for k in range(CHUNKS):
        tb[2 * k : 2 * k + 2, :] = stream[:, KC * k : KC * k + KC]
    fill_gain(gain1)
    lane2 = iota((2, KC), 1)
    combine = jnp.zeros((2, KC), F32)
    chosen = ids[...]
    weights = wts[...]
    for k in range(TOP):
        combine += jnp.where(chosen[:, k : k + 1] == lax.rem(lane2, EXPERTS), weights[:, k : k + 1], 0.0)
    high = rounded(combine)
    ab[...] = jnp.zeros((16, KC), F32)
    ab[14:16, :] = jnp.where(
        lane2 < EXPERTS, high, jnp.where(lane2 < 2 * EXPERTS, combine - high, 0.0)
    )

    def gather(layer, block, side):
        place_rows = chunk_rows(a2)
        mine = gath.at[layer, 0, place_rows, :]
        gath[layer, 0, place_rows, :] = jnp.where(
            row < 2 * CHUNKS, block * gb[...], side
        ).astype(BF16)
        if layer == 0:
            pl.semaphore_wait(barrier, 2 * (N - 1) + NX)
        first = [
            send(mine, mine, ag1_s.at[layer, d], ag1_r.at[layer, d], peer2(d)) for d in FAR
        ]
        for copy in first:
            copy.start()
        for copy in first:
            copy.wait_recv()
        line = gath.at[layer, 0]
        second = {}
        for d in FAR:
            second[d] = send(
                line, gath.at[layer, d], ag2_s.at[layer, d], ag2_r.at[layer, d], peer1(d)
            )
            second[d].start()
        forwards = {0: forward(layer, 0)}
        return first, second, forwards

    def forward(layer, d):
        copy = send(
            gath.at[layer, d],
            gath.at[layer, N + d],
            fw_s.at[layer, d],
            fw_r.at[layer, d],
            sibling,
        )
        copy.start()
        return copy

    def permuted(layer, batch, other):
        groups = [gath[layer, N * other + d] for d in BATCHES[batch]]
        moved = jnp.dot(
            perm[...], jnp.concatenate(groups, axis=1), preferred_element_type=F32
        ).astype(BF16)
        for q in range(len(groups)):
            start = HALF * batch + 64 * other + 16 * q
            for k in range(CHUNKS + 1):
                xm[start : start + 16, KC * k : KC * k + KC] = moved[
                    16 * k : 16 * k + 16, KC * q : KC * q + KC
                ]

    def receive(layer, batch, second, forwards):
        for d in BATCHES[batch]:
            if d:
                second[d].wait_recv()
                forwards[d] = forward(layer, d)
        permuted(layer, batch, 0)
        for d in BATCHES[batch]:
            forwards[d].wait_recv()
        permuted(layer, batch, 1)

    def part_rows(batch, index):
        return pl.ds(pl.multiple_of(batch * HALF + index * XR, XR), XR)

    def project(layer, batch, px, rx, weight):
        rows = pl.ds(batch * HALF, HALF)
        px[rows, :] = lax.dot_general(
            xm[rows, :],
            weight[...],
            (((1,), (1 - layer,)), ((), ())),
            preferred_element_type=F32,
        ).astype(BF16)
        copies = [
            send(
                px.at[part_rows(batch, lax.rem(x + d, NX)), :],
                rx.at[batch, d],
                rx_s.at[layer, batch, d],
                rx_r.at[layer, batch, d],
                peerx(d),
            )
            for d in (2, 1, 3)
        ]
        for copy in copies:
            copy.start()
        if layer == 0:
            cw[rows, :] = jnp.dot(xm[rows, DL:], selector, preferred_element_type=F32)
        return copies

    def activate(layer, batch, px, rx, copies):
        rows = part_rows(batch, x)
        total = px[rows, :].astype(F32)
        for copy, d in zip(copies, (2, 1, 3)):
            copy.wait_recv()
            total = total + rx[batch, d].astype(F32)
        tail = total[:, total.shape[1] - 128 :]
        spot = iota((XR, 128), 1)
        if layer == 0:
            used = (spot >= 96) & (spot < 99)
        else:
            used = spot < 3
        squares = jnp.sum(jnp.where(used, tail, 0.0), axis=1, keepdims=True)
        scale = lax.rsqrt(squares / D + 1e-06)
        if layer == 0:
            main = jax.nn.silu(total[:, :128] * scale) * (total[:, 128:256] * scale)
            last = jax.nn.silu(tail * scale) * (pltpu.roll(tail, 64, 1) * scale)
            last = jnp.where(spot < 16, last, 0.0)
            value = jnp.concatenate((main, last), axis=1)
        else:
            value = jax.nn.silu(total[:, :256] * scale) * (total[:, 256:512] * scale)
            share = cw[rows, :]
            value = value * jnp.concatenate((share, share), axis=1)
        hid[layer, rows, :] = value.astype(BF16)
        mine = hid.at[layer, rows, :]
        out_copies = [
            send(
                mine,
                mine,
                hx_s.at[layer, batch, d],
                hx_r.at[layer, batch, d],
                peerx(d),
            )
            for d in (2, 1, 3)
        ]
        for copy in out_copies:
            copy.start()
        return out_copies

    def lower(layer, batch, weight, copies):
        for copy in copies:
            copy.wait_recv()
        value = hid[layer, HALF * batch : HALF * batch + HALF, :]
        rows = pl.ds(64 * batch, 64)
        for k in range(CHUNKS):
            part = jnp.dot(value, weight[:, KC * k : KC * k + KC], preferred_element_type=F32)
            of[rows, KC * k : KC * k + KC] = part[:64, :]
            cs[layer, rows, KC * k : KC * k + KC] = part[64:, :].astype(BF16)
        cross = []
        for q, d in enumerate(BATCHES[batch]):
            part_of = pl.ds(64 * batch + 16 * q, 16)
            cross.append(
                send(
                    cs.at[layer, part_of, :],
                    cr.at[layer, part_of, :],
                    co_s.at[layer, d],
                    co_r.at[layer, d],
                    sibling,
                )
            )
            cross[q].start()
        return cross

    def chunk_rows(index):
        return pl.ds(pl.multiple_of(index * 16, 16), 16)

    def scatter(layer, batch, cross):
        sent = {}
        for q, d in enumerate(BATCHES[batch]):
            rows = pl.ds(64 * batch + 16 * q, 16)
            cross[q].wait_recv()
            value = of[rows, :] + cr[layer, rows, :].astype(F32)
            s1[layer, rows, :] = value.astype(BF16)
            if d:
                sent[d] = send(
                    s1.at[layer, rows, :],
                    r1.at[layer, d],
                    r1_s.at[layer, d],
                    r1_r.at[layer, d],
                    peer1(N - d),
                )
                sent[d].start()
            else:
                r1[layer, 0] = value.astype(BF16)
        return sent

    def collect(layer, first):
        total = r1[layer, 0].astype(F32)
        for d in FAR:
            first[d].wait_recv()
            total = total + r1[layer, d].astype(F32)
        total = total.astype(BF16)
        stacked = jnp.concatenate(
            [total[:, KC * k : KC * k + KC] for k in range(CHUNKS)] + [jnp.zeros((16, KC), BF16)],
            axis=0,
        )
        s2[layer] = jnp.dot(perm[...], stacked, preferred_element_type=F32).astype(BF16)
        second = {}
        for d in FAR:
            second[d] = send(
                s2.at[layer, chunk_rows(lax.rem(a2 + d, N)), :],
                r2.at[layer, d],
                r2_s.at[layer, d],
                r2_r.at[layer, d],
                peer2(d),
            )
            second[d].start()
        total = s2[layer, chunk_rows(a2), :].astype(F32)
        for d in NEAR:
            second[d].wait_recv()
            total = total + r2[layer, d].astype(F32)
        return total, second

    def layer_of(layer, block, side, px, rx, w_in, w_out, loads_in, loads_out):
        first, second, forwards = gather(layer, block, side)
        receive(layer, 0, second, forwards)
        for load in loads_in:
            load.wait()
        x0 = project(layer, 0, px, rx, w_in)
        receive(layer, 1, second, forwards)
        x1 = project(layer, 1, px, rx, w_in)
        h0 = activate(layer, 0, px, rx, x0)
        h1 = activate(layer, 1, px, rx, x1)
        for load in loads_out:
            load.wait()
        c0 = lower(layer, 0, w_out, h0)
        sent = scatter(layer, 0, c0)
        c1 = lower(layer, 1, w_out, h1)
        sent.update(scatter(layer, 1, c1))
        total, last = collect(layer, sent)
        started = first + x0 + x1 + h0 + h1 + c0 + c1
        for group in (second, forwards, sent, last):
            started += group.values()
        return total, started

    expert = dp // (EH // 256)
    at = iota((KC, 128), 0)
    selector = ((at == expert) | (at == expert + EXPERTS)).astype(F32).astype(BF16)

    to = iota((128, 128), 0)
    source = lax.rem(to // 2, 8) * 16 + (to // 16) * 2 + lax.rem(to, 2)
    perm[...] = (source == iota((128, 128), 1)).astype(F32).astype(BF16)
    side_row = iota((KC, 128), 0)
    side_lane = iota((KC, 128), 1)
    is_part = (side_row >= 32) & (side_row < 35)
    w1[:256, DL:] = jnp.zeros((256, KC), BF16)
    w1[272:320, :DL] = jnp.zeros((48, DL), BF16)
    w1[336:, :DL] = jnp.zeros((48, DL), BF16)
    to_row = iota((128, KC), 0)
    to_lane = iota((128, KC), 1)
    wanted = (to_lane >= 32) & (to_lane < 35) & (to_row == to_lane + 64)
    w1[256:, DL:] = wanted.astype(F32).astype(BF16)
    w2[144:, :] = jnp.zeros((112, DL), BF16)
    w3[DL:, :512] = jnp.zeros((KC, 512), BF16)
    w3[:DL, 512:] = jnp.zeros((DL, 128), BF16)
    w3[DL:, 512:] = (is_part & (side_lane == side_row - 32)).astype(F32).astype(BF16)

    tokens_block = tb[...]
    side = jnp.where(row >= 14, ab[...] + sums_of_squares(tokens_block), 0.0)
    dense, pending = layer_of(
        0, tokens_block, side, px0, rx0, w1, w2, loads[0:4], loads[4:5]
    )
    fill_gain(gain2)
    mixed = rounded(tb[...] + dense)
    mixed = jnp.where(row < 2 * CHUNKS, mixed, 0.0)
    tb[...] = mixed
    side = jnp.where(row >= 14, sums_of_squares(mixed), 0.0)
    routed, more = layer_of(
        1, mixed, side, px1, rx1, w3, w4, loads[5:7], loads[7:]
    )
    tb[...] = tb[...] + routed
    live = iota((2, KC), 0) < newt[0]
    for k in range(CHUNKS):
        out[:, KC * k : KC * k + KC] = jnp.where(live, tb[2 * k : 2 * k + 2, :], 0.0)
    for copy in pending + more:
        copy.wait_send()


def shards(
    tokens,
    new_tokens,
    dense_gain,
    dense_gate,
    dense_up,
    dense_down,
    moe_gain,
    expert_ids,
    expert_weights,
    expert_gate,
    expert_up,
    expert_down,
):
    vmem = pl.BlockSpec(memory_space=pltpu.VMEM)
    smem = pl.BlockSpec(memory_space=pltpu.SMEM)
    anywhere = pl.BlockSpec(memory_space=pltpu.HBM)
    sems = pltpu.SemaphoreType.DMA
    result = pl.pallas_call(
        kernel,
        out_shape=jax.ShapeDtypeStruct((2, DL), F32),
        in_specs=[
            vmem,
            smem,
            vmem,
            anywhere,
            anywhere,
            anywhere,
            vmem,
            vmem,
            vmem,
            anywhere,
            anywhere,
            anywhere,
        ],
        out_specs=vmem,
        scratch_shapes=[
            pltpu.VMEM((384, DL + KC), BF16),
            pltpu.VMEM((256, DL), BF16),
            pltpu.VMEM((DL + KC, 640), BF16),
            pltpu.VMEM((256, DL), BF16),
            pltpu.VMEM((16, KC), F32),
            pltpu.VMEM((16, KC), F32),
            pltpu.VMEM((16, KC), F32),
            pltpu.VMEM((128, 128), BF16),
            pltpu.VMEM((2, 2 * N, 128, KC), BF16),
            pltpu.VMEM((2 * HALF, DL + KC), BF16),
            pltpu.VMEM((2 * HALF, 128), F32),
            pltpu.VMEM((2 * HALF, 384), BF16),
            pltpu.VMEM((2 * HALF, 640), BF16),
            pltpu.VMEM((2, NX, XR, 384), BF16),
            pltpu.VMEM((2, NX, XR, 640), BF16),
            pltpu.VMEM((2, 2 * HALF, 256), BF16),
            pltpu.VMEM((2, HALF, DL), BF16),
            pltpu.VMEM((2, HALF, DL), BF16),
            pltpu.VMEM((HALF, DL), F32),
            pltpu.VMEM((2, HALF, DL), BF16),
            pltpu.VMEM((2, N, 16, DL), BF16),
            pltpu.VMEM((2, 128, KC), BF16),
            pltpu.VMEM((2, N, 16, KC), BF16),
            sems((8,)),
            sems((2, N)),
            sems((2, N)),
            sems((2, N)),
            sems((2, N)),
            sems((2, N)),
            sems((2, N)),
            sems((2, 2, NX)),
            sems((2, 2, NX)),
            sems((2, 2, NX)),
            sems((2, 2, NX)),
            sems((2, N)),
            sems((2, N)),
            sems((2, N)),
            sems((2, N)),
            sems((2, N)),
            sems((2, N)),
        ],
        compiler_params=pltpu.CompilerParams(
            collective_id=0, has_side_effects=True, vmem_limit_bytes=60 * 1024 * 1024
        ),
        name="layers",
    )(
        tokens,
        new_tokens,
        dense_gain,
        dense_gate.T,
        dense_up.T,
        dense_down,
        moe_gain,
        expert_ids,
        expert_weights,
        expert_gate,
        expert_up,
        expert_down,
    )
    return result.astype(BF16)


def solution(mesh):
    placed = (
        P("dp", "sub"),
        P("dp"),
        P("sub"),
        P("sub", "dp"),
        P("sub", "dp"),
        P("dp", "sub"),
        P("sub"),
        P("dp", None),
        P("dp", None),
        P("sub", "dp"),
        P("sub", "dp"),
        P("dp", "sub"),
    )
    return jax.shard_map(
        shards, mesh=mesh, in_specs=placed, out_specs=P("dp", "sub"), check_vma=False
    )
```

```python
import functools

import jax
import jax.numpy as jnp
from jax import lax
from jax.experimental import pallas as pl
from jax.experimental.pallas import tpu as pltpu
from jax.sharding import PartitionSpec as P

D = 7168
EH = 2048
EXPERTS = 16
TOP = 8
N = 8
NX = 4
DL = 1792
KC = 256
CHUNKS = DL // KC
HALF = 128
MESH = pl.DeviceIdType.MESH
F32 = jnp.float32
BF16 = jnp.bfloat16
FAR = (4, 3, 5, 2, 6, 1, 7)
NEAR = (1, 7, 2, 6, 3, 5, 4)
BATCHES = ((4, 3, 5, 0), (2, 6, 1, 7))
FIRST = (4, 3, 5)
LATER = (2, 6, 1, 7)
EARLY = 1
STEPS = ("r0", "r1", "a0", "a1", "l0", "s0", "l1", "s1")
START = tuple(sum(len(b) for b in BATCHES[:i]) for i in range(len(BATCHES)))
XR = tuple(8 * len(b) for b in BATCHES)


def iota(shape, dim):
    return lax.broadcasted_iota(jnp.int32, shape, dim)


def rounded(value):
    return value.astype(BF16).astype(F32)


def kernel(
    tok_in,
    newt,
    gain1_in,
    gate,
    up,
    down,
    gain2_in,
    ids_in,
    wts_in,
    egate,
    eup,
    edown,
    out,
    tok,
    gain1,
    gain2,
    ids,
    wts,
    w1,
    w2,
    w3,
    w4,
    tb,
    gb,
    ab,
    perm,
    gath,
    xm,
    cw,
    px0,
    px1,
    rx0,
    rx1,
    hid,
    cs,
    cr,
    of,
    s1,
    r1,
    s2,
    r2,
    ssem,
    wsem,
    ag1_s,
    ag1_r,
    ag2_s,
    ag2_r,
    fw_s,
    fw_r,
    rx_s,
    rx_r,
    hx_s,
    hx_r,
    co_s,
    co_r,
    r1_s,
    r1_r,
    r2_s,
    r2_r,
):
    dp = lax.axis_index("dp")
    x = lax.axis_index("sub")
    c = lax.rem(dp, 2)
    y = dp // (2 * N)
    z = lax.rem(dp // 2, N)
    a1 = y * (1 - c) + z * c
    a2 = z * (1 - c) + y * c

    def place(i1, i2):
        return (((i1 * N + i2) * (1 - c) + (i2 * N + i1) * c) * 2 + c, x)

    def peer1(d):
        return place(lax.rem(a1 + d, N), a2)

    def peer2(d):
        return place(a1, lax.rem(a2 + d, N))

    def peerx(d):
        return (dp, lax.rem(x + d, NX))

    sibling = (dp + 1 - 2 * c, x)

    def send(src, dst, ssem, rsem, device):
        return pltpu.make_async_remote_copy(
            src_ref=src,
            dst_ref=dst,
            send_sem=ssem,
            recv_sem=rsem,
            device_id=device,
            device_id_type=MESH,
        )

    barrier = pltpu.get_barrier_semaphore()
    for d in range(1, N):
        pl.semaphore_signal(barrier, inc=1, device_id=peer2(d), device_id_type=MESH)
        pl.semaphore_signal(barrier, inc=1, device_id=peer1(d), device_id_type=MESH)
    for d in range(1, NX):
        pl.semaphore_signal(barrier, inc=1, device_id=peerx(d), device_id_type=MESH)
    pl.semaphore_signal(barrier, inc=1, device_id=sibling, device_id_type=MESH)

    small = [
        pltpu.make_async_copy(src, dst, ssem.at[i])
        for i, (src, dst) in enumerate(
            (
                (tok_in, tok),
                (gain1_in, gain1),
                (ids_in, ids),
                (wts_in, wts),
                (gain2_in, gain2),
            )
        )
    ]
    for load in small:
        load.start()
    loads = [
        pltpu.make_async_copy(src, dst, wsem.at[i])
        for i, (src, dst) in enumerate(
            (
                (gate.at[pl.ds(0, 128), :], w1.at[pl.ds(0, 128), pl.ds(0, DL)]),
                (up.at[pl.ds(0, 128), :], w1.at[pl.ds(128, 128), pl.ds(0, DL)]),
                (gate.at[pl.ds(128, 16), :], w1.at[pl.ds(256, 16), pl.ds(0, DL)]),
                (up.at[pl.ds(128, 16), :], w1.at[pl.ds(320, 16), pl.ds(0, DL)]),
                (down, w2.at[pl.ds(0, 144), :]),
                (egate, w3.at[pl.ds(0, DL), pl.ds(0, 256)]),
                (eup, w3.at[pl.ds(0, DL), pl.ds(256, 256)]),
                (edown, w4),
            )
        )
    ]
    for load in loads:
        load.start()

    row = iota((16, KC), 0)
    lane = iota((16, KC), 1)
    odd = lax.rem(row, 2) == 1

    def sums_of_squares(block):
        each = jnp.sum(block * block, axis=1, keepdims=True)
        each = jnp.broadcast_to(each, (16, KC))
        even_sum = jnp.sum(jnp.where(odd, 0.0, each), axis=0, keepdims=True)
        odd_sum = jnp.sum(jnp.where(odd, each, 0.0), axis=0, keepdims=True)
        total = jnp.where(odd, odd_sum, even_sum)
        high = rounded(total)
        middle = rounded(total - high)
        low = total - high - middle
        return jnp.where(
            lane == 32, high, jnp.where(lane == 33, middle, jnp.where(lane == 34, low, 0.0))
        )

    def fill_gain(gain):
        gb[...] = jnp.zeros((16, KC), F32)
        for k in range(CHUNKS):
            gb[2 * k : 2 * k + 2, :] = jnp.broadcast_to(gain[KC * k : KC * k + KC][None, :], (2, KC))

    for load in small:
        load.wait()
    stream = tok[...].astype(F32)
    tb[...] = jnp.zeros((16, KC), F32)
    for k in range(CHUNKS):
        tb[2 * k : 2 * k + 2, :] = stream[:, KC * k : KC * k + KC]
    fill_gain(gain1)
    lane2 = iota((2, KC), 1)
    combine = jnp.zeros((2, KC), F32)
    chosen = ids[...]
    weights = wts[...]
    for k in range(TOP):
        combine += jnp.where(chosen[:, k : k + 1] == lax.rem(lane2, EXPERTS), weights[:, k : k + 1], 0.0)
    high = rounded(combine)
    ab[...] = jnp.zeros((16, KC), F32)
    ab[14:16, :] = jnp.where(
        lane2 < EXPERTS, high, jnp.where(lane2 < 2 * EXPERTS, combine - high, 0.0)
    )

    def gather(layer, block, side, earlier):
        place_rows = chunk_rows(a2)
        mine = gath.at[layer, 0, place_rows, :]
        gath[layer, 0, place_rows, :] = jnp.where(
            row < 2 * CHUNKS, block * gb[...], side
        ).astype(BF16)
        if layer == 0:
            pl.semaphore_wait(barrier, 2 * (N - 1) + NX)
        first = [
            send(mine, mine, ag1_s.at[layer, d], ag1_r.at[layer, d], peer2(d)) for d in FAR
        ]
        for copy in first:
            copy.start()
        line = gath.at[layer, 0]
        second = {
            d: send(line, gath.at[layer, d], ag2_s.at[layer, d], ag2_r.at[layer, d], peer1(d))
            for d in FAR
        }

        def pass_on(rows, offsets):
            for d in offsets:
                send(
                    gath.at[layer, 0, rows, :],
                    gath.at[layer, d, rows, :],
                    ag2_s.at[layer, d],
                    ag2_r.at[layer, d],
                    peer1(d),
                ).start()

        pass_on(place_rows, FIRST + LATER)
        if layer == 0:
            fill()
        else:
            for copy in earlier:
                copy.wait_send()
        held = []
        for i, copy in enumerate(reversed(first)):
            copy.wait_recv()
            rows = chunk_rows(lax.rem(a2 + N - FAR[N - 2 - i], N))
            pass_on(rows, FIRST)
            if i + 1 < EARLY:
                pass_on(rows, LATER)
            else:
                held.append(rows)
        for rows in held:
            pass_on(rows, LATER)
        forwards = {0: forward(layer, 0)}
        return first, second, forwards

    def forward(layer, d):
        copy = send(
            gath.at[layer, d],
            gath.at[layer, N + d],
            fw_s.at[layer, d],
            fw_r.at[layer, d],
            sibling,
        )
        copy.start()
        return copy

    def permuted(layer, batch, other):
        groups = [gath[layer, N * other + d] for d in BATCHES[batch]]
        moved = jnp.dot(
            perm[...], jnp.concatenate(groups, axis=1), preferred_element_type=F32
        ).astype(BF16)
        for q in range(len(groups)):
            start = 32 * START[batch] + 16 * len(groups) * other + 16 * q
            for k in range(CHUNKS + 1):
                xm[start : start + 16, KC * k : KC * k + KC] = moved[
                    16 * k : 16 * k + 16, KC * q : KC * q + KC
                ]

    def receive(layer, batch, second, forwards):
        for d in BATCHES[batch]:
            if d:
                second[d].wait_recv()
                forwards[d] = forward(layer, d)
        permuted(layer, batch, 0)
        for d in BATCHES[batch]:
            forwards[d].wait_recv()
        permuted(layer, batch, 1)

    def part_rows(batch, index):
        return pl.ds(
            pl.multiple_of(32 * START[batch] + index * XR[batch], XR[batch]), XR[batch]
        )

    def batch_rows(batch):
        return pl.ds(32 * START[batch], 32 * len(BATCHES[batch]))

    def project(layer, batch, px, rx, weight):
        rows = batch_rows(batch)
        px[rows, :] = lax.dot_general(
            xm[rows, :],
            weight[...],
            (((1,), (1 - layer,)), ((), ())),
            preferred_element_type=F32,
        ).astype(BF16)
        copies = [
            send(
                px.at[part_rows(batch, lax.rem(x + d, NX)), :],
                rx.at[d, pl.ds(8 * START[batch], XR[batch]), :],
                rx_s.at[layer, batch, d],
                rx_r.at[layer, batch, d],
                peerx(d),
            )
            for d in (2, 1, 3)
        ]
        for copy in copies:
            copy.start()
        if layer == 0:
            cw[rows, :] = jnp.dot(xm[rows, DL:], selector, preferred_element_type=F32)
        return copies

    def activate(layer, batch, px, rx, copies):
        rows = part_rows(batch, x)
        total = px[rows, :].astype(F32)
        for copy, d in zip(copies, (2, 1, 3)):
            copy.wait_recv()
            total = total + rx[d, pl.ds(8 * START[batch], XR[batch]), :].astype(F32)
        tail = total[:, total.shape[1] - 128 :]
        spot = iota((XR[batch], 128), 1)
        if layer == 0:
            used = (spot >= 96) & (spot < 99)
        else:
            used = spot < 3
        squares = jnp.sum(jnp.where(used, tail, 0.0), axis=1, keepdims=True)
        scale = lax.rsqrt(squares / D + 1e-06)
        if layer == 0:
            main = jax.nn.silu(total[:, :128] * scale) * (total[:, 128:256] * scale)
            last = jax.nn.silu(tail * scale) * (pltpu.roll(tail, 64, 1) * scale)
            last = jnp.where(spot < 16, last, 0.0)
            value = jnp.concatenate((main, last), axis=1)
        else:
            value = jax.nn.silu(total[:, :256] * scale) * (total[:, 256:512] * scale)
            share = cw[rows, :]
            value = value * jnp.concatenate((share, share), axis=1)
        hid[layer, rows, :] = value.astype(BF16)
        mine = hid.at[layer, rows, :]
        out_copies = [
            send(
                mine,
                mine,
                hx_s.at[layer, batch, d],
                hx_r.at[layer, batch, d],
                peerx(d),
            )
            for d in (2, 1, 3)
        ]
        for copy in out_copies:
            copy.start()
        return out_copies

    def lower(layer, batch, weight, copies):
        for copy in copies:
            copy.wait_recv()
        value = hid[layer, batch_rows(batch), :]
        count = 16 * len(BATCHES[batch])
        rows = pl.ds(16 * START[batch], count)
        for k in range(CHUNKS):
            part = jnp.dot(value, weight[:, KC * k : KC * k + KC], preferred_element_type=F32)
            of[rows, KC * k : KC * k + KC] = part[:count, :]
            cs[layer, rows, KC * k : KC * k + KC] = part[count:, :].astype(BF16)
        cross = []
        for q, d in enumerate(BATCHES[batch]):
            part_of = pl.ds(16 * START[batch] + 16 * q, 16)
            cross.append(
                send(
                    cs.at[layer, part_of, :],
                    cr.at[layer, part_of, :],
                    co_s.at[layer, d],
                    co_r.at[layer, d],
                    sibling,
                )
            )
            cross[q].start()
        return cross

    def chunk_rows(index):
        return pl.ds(pl.multiple_of(index * 16, 16), 16)

    def scatter(layer, batch, cross):
        sent = {}
        for q, d in enumerate(BATCHES[batch]):
            rows = pl.ds(16 * START[batch] + 16 * q, 16)
            cross[q].wait_recv()
            value = of[rows, :] + cr[layer, rows, :].astype(F32)
            s1[layer, rows, :] = value.astype(BF16)
            if d:
                sent[d] = send(
                    s1.at[layer, rows, :],
                    r1.at[layer, d],
                    r1_s.at[layer, d],
                    r1_r.at[layer, d],
                    peer1(N - d),
                )
                sent[d].start()
            else:
                r1[layer, 0] = value.astype(BF16)
        return sent

    def collect(layer, first, started):
        total = r1[layer, 0].astype(F32)
        for d in FAR:
            first[d].wait_recv()
            total = total + r1[layer, d].astype(F32)
        total = total.astype(BF16)
        stacked = jnp.concatenate(
            [total[:, KC * k : KC * k + KC] for k in range(CHUNKS)] + [jnp.zeros((16, KC), BF16)],
            axis=0,
        )
        s2[layer] = jnp.dot(perm[...], stacked, preferred_element_type=F32).astype(BF16)
        second = {}
        for d in FAR:
            second[d] = send(
                s2.at[layer, chunk_rows(lax.rem(a2 + d, N)), :],
                r2.at[layer, d],
                r2_s.at[layer, d],
                r2_r.at[layer, d],
                peer2(d),
            )
            second[d].start()
        for copy in started:
            copy.wait_send()
        total = s2[layer, chunk_rows(a2), :].astype(F32)
        for d in NEAR:
            second[d].wait_recv()
            total = total + r2[layer, d].astype(F32)
        return total, list(second.values())

    def layer_of(layer, block, side, px, rx, w_in, w_out, loads_in, loads_out, earlier):
        first, second, forwards = gather(layer, block, side, earlier)
        parts, hiddens, crossed, sent = {}, {}, {}, {}
        for step in STEPS:
            b = int(step[1])
            if step == "r0":
                receive(layer, b, second, forwards)
                for load in loads_in:
                    load.wait()
                parts[b] = project(layer, b, px, rx, w_in)
            elif step[0] == "r":
                receive(layer, b, second, forwards)
                parts[b] = project(layer, b, px, rx, w_in)
            elif step[0] == "a":
                hiddens[b] = activate(layer, b, px, rx, parts[b])
            elif step[0] == "l":
                if b == 0:
                    for load in loads_out:
                        load.wait()
                crossed[b] = lower(layer, b, w_out, hiddens[b])
            else:
                sent.update(scatter(layer, b, crossed[b]))
        started = list(first)
        for group in (parts, hiddens, crossed):
            started += [copy for copies in group.values() for copy in copies]
        for group in (second, forwards, sent):
            started += group.values()
        return collect(layer, sent, started)

    expert = dp // (EH // 256)
    at = iota((KC, 128), 0)
    selector = ((at == expert) | (at == expert + EXPERTS)).astype(F32).astype(BF16)

    def fill():
        to = iota((128, 128), 0)
        source = lax.rem(to // 2, 8) * 16 + (to // 16) * 2 + lax.rem(to, 2)
        perm[...] = (source == iota((128, 128), 1)).astype(F32).astype(BF16)
        side_row = iota((KC, 128), 0)
        side_lane = iota((KC, 128), 1)
        is_part = (side_row >= 32) & (side_row < 35)
        w1[:256, DL:] = jnp.zeros((256, KC), BF16)
        w1[272:320, :DL] = jnp.zeros((48, DL), BF16)
        w1[336:, :DL] = jnp.zeros((48, DL), BF16)
        to_row = iota((128, KC), 0)
        to_lane = iota((128, KC), 1)
        wanted = (to_lane >= 32) & (to_lane < 35) & (to_row == to_lane + 64)
        w1[256:, DL:] = wanted.astype(F32).astype(BF16)
        w2[144:, :] = jnp.zeros((112, DL), BF16)
        w3[DL:, :512] = jnp.zeros((KC, 512), BF16)
        w3[:DL, 512:] = jnp.zeros((DL, 128), BF16)
        w3[DL:, 512:] = (is_part & (side_lane == side_row - 32)).astype(F32).astype(BF16)

    tokens_block = tb[...]
    side = jnp.where(row >= 14, ab[...] + sums_of_squares(tokens_block), 0.0)
    dense, pending = layer_of(
        0, tokens_block, side, px0, rx0, w1, w2, loads[0:4], loads[4:5], ()
    )
    fill_gain(gain2)
    mixed = rounded(tb[...] + dense)
    mixed = jnp.where(row < 2 * CHUNKS, mixed, 0.0)
    tb[...] = mixed
    side = jnp.where(row >= 14, sums_of_squares(mixed), 0.0)
    routed, more = layer_of(
        1, mixed, side, px1, rx1, w3, w4, loads[5:7], loads[7:], pending
    )
    tb[...] = tb[...] + routed
    live = iota((2, KC), 0) < newt[0]
    for k in range(CHUNKS):
        out[:, KC * k : KC * k + KC] = jnp.where(live, tb[2 * k : 2 * k + 2, :], 0.0)
    for copy in more:
        copy.wait_send()


def shards(
    tokens,
    new_tokens,
    dense_gain,
    dense_gate,
    dense_up,
    dense_down,
    moe_gain,
    expert_ids,
    expert_weights,
    expert_gate,
    expert_up,
    expert_down,
):
    vmem = pl.BlockSpec(memory_space=pltpu.VMEM)
    smem = pl.BlockSpec(memory_space=pltpu.SMEM)
    anywhere = pl.BlockSpec(memory_space=pltpu.HBM)
    sems = pltpu.SemaphoreType.DMA
    result = pl.pallas_call(
        kernel,
        out_shape=jax.ShapeDtypeStruct((2, DL), F32),
        in_specs=[anywhere, smem] + [anywhere] * 10,
        out_specs=vmem,
        scratch_shapes=[
            pltpu.VMEM((2, DL), BF16),
            pltpu.VMEM((DL,), F32),
            pltpu.VMEM((DL,), F32),
            pltpu.VMEM((2, TOP), jnp.int32),
            pltpu.VMEM((2, TOP), F32),
            pltpu.VMEM((384, DL + KC), BF16),
            pltpu.VMEM((256, DL), BF16),
            pltpu.VMEM((DL + KC, 640), BF16),
            pltpu.VMEM((256, DL), BF16),
            pltpu.VMEM((16, KC), F32),
            pltpu.VMEM((16, KC), F32),
            pltpu.VMEM((16, KC), F32),
            pltpu.VMEM((128, 128), BF16),
            pltpu.VMEM((2, 2 * N, 128, KC), BF16),
            pltpu.VMEM((2 * HALF, DL + KC), BF16),
            pltpu.VMEM((2 * HALF, 128), F32),
            pltpu.VMEM((2 * HALF, 384), BF16),
            pltpu.VMEM((2 * HALF, 640), BF16),
            pltpu.VMEM((NX, 64, 384), BF16),
            pltpu.VMEM((NX, 64, 640), BF16),
            pltpu.VMEM((2, 2 * HALF, 256), BF16),
            pltpu.VMEM((2, HALF, DL), BF16),
            pltpu.VMEM((2, HALF, DL), BF16),
            pltpu.VMEM((HALF, DL), F32),
            pltpu.VMEM((2, HALF, DL), BF16),
            pltpu.VMEM((2, N, 16, DL), BF16),
            pltpu.VMEM((2, 128, KC), BF16),
            pltpu.VMEM((2, N, 16, KC), BF16),
            sems((5,)),
            sems((8,)),
            sems((2, N)),
            sems((2, N)),
            sems((2, N)),
            sems((2, N)),
            sems((2, N)),
            sems((2, N)),
            sems((2, len(BATCHES), NX)),
            sems((2, len(BATCHES), NX)),
            sems((2, len(BATCHES), NX)),
            sems((2, len(BATCHES), NX)),
            sems((2, N)),
            sems((2, N)),
            sems((2, N)),
            sems((2, N)),
            sems((2, N)),
            sems((2, N)),
        ],
        compiler_params=pltpu.CompilerParams(
            collective_id=0, has_side_effects=True, vmem_limit_bytes=60 * 1024 * 1024
        ),
        name="layers",
    )(
        tokens,
        new_tokens,
        dense_gain,
        dense_gate.T,
        dense_up.T,
        dense_down,
        moe_gain,
        expert_ids,
        expert_weights,
        expert_gate,
        expert_up,
        expert_down,
    )
    return result.astype(BF16)


def solution(mesh):
    placed = (
        P("dp", "sub"),
        P("dp"),
        P("sub"),
        P("sub", "dp"),
        P("sub", "dp"),
        P("dp", "sub"),
        P("sub"),
        P("dp", None),
        P("dp", None),
        P("sub", "dp"),
        P("sub", "dp"),
        P("dp", "sub"),
    )
    return jax.shard_map(
        shards, mesh=mesh, in_specs=placed, out_specs=P("dp", "sub"), check_vma=False
    )
```

```python
import functools

import jax
import jax.numpy as jnp
from jax import lax
from jax.experimental import pallas as pl
from jax.experimental.pallas import tpu as pltpu
from jax.sharding import PartitionSpec as P

D = 7168
EH = 2048
EXPERTS = 16
TOP = 8
N = 8
NX = 4
DL = 1792
KC = 256
CHUNKS = DL // KC
HALF = 128
MESH = pl.DeviceIdType.MESH
F32 = jnp.float32
BF16 = jnp.bfloat16
FAR = (4, 3, 5, 2, 6, 1, 7)
NEAR = (1, 7, 2, 6, 3, 5, 4)
BATCHES = ((4, 3, 5, 0), (2, 6, 1, 7))
FIRST = (4, 3, 5)
LATER = (2, 6, 1, 7)
EARLY = 1
STEPS = ("r0", "r1", "a0", "a1", "l0", "s0", "l1", "s1")
START = tuple(sum(len(b) for b in BATCHES[:i]) for i in range(len(BATCHES)))
XR = tuple(8 * len(b) for b in BATCHES)


def iota(shape, dim):
    return lax.broadcasted_iota(jnp.int32, shape, dim)


def rounded(value):
    return value.astype(BF16).astype(F32)


def kernel(
    tok_in,
    newt,
    gain1_in,
    gate,
    up,
    down,
    gain2_in,
    ids_in,
    wts_in,
    egate,
    eup,
    edown,
    out,
    tok,
    gain1,
    gain2,
    ids,
    wts,
    w1,
    w2,
    w3,
    w4,
    tb,
    gb,
    ab,
    perm,
    gath,
    xm,
    cw,
    px0,
    px1,
    rx0,
    rx1,
    hid,
    cs,
    cr,
    of,
    s1,
    r1,
    s2,
    r2,
    ssem,
    wsem,
    ag1_s,
    ag1_r,
    ag2_s,
    ag2_r,
    fw_s,
    fw_r,
    rx_s,
    rx_r,
    hx_s,
    hx_r,
    co_s,
    co_r,
    r1_s,
    r1_r,
    r2_s,
    r2_r,
):
    dp = lax.axis_index("dp")
    x = lax.axis_index("sub")
    c = lax.rem(dp, 2)
    y = dp // (2 * N)
    z = lax.rem(dp // 2, N)
    a1 = y * (1 - c) + z * c
    a2 = z * (1 - c) + y * c

    def place(i1, i2):
        return (((i1 * N + i2) * (1 - c) + (i2 * N + i1) * c) * 2 + c, x)

    def peer1(d):
        return place(lax.rem(a1 + d, N), a2)

    def peer2(d):
        return place(a1, lax.rem(a2 + d, N))

    def peerx(d):
        return (dp, lax.rem(x + d, NX))

    sibling = (dp + 1 - 2 * c, x)

    def send(src, dst, ssem, rsem, device):
        return pltpu.make_async_remote_copy(
            src_ref=src,
            dst_ref=dst,
            send_sem=ssem,
            recv_sem=rsem,
            device_id=device,
            device_id_type=MESH,
        )

    barrier = pltpu.get_barrier_semaphore()
    for d in range(1, N):
        pl.semaphore_signal(barrier, inc=1, device_id=peer2(d), device_id_type=MESH)
        pl.semaphore_signal(barrier, inc=1, device_id=peer1(d), device_id_type=MESH)
    for d in range(1, NX):
        pl.semaphore_signal(barrier, inc=1, device_id=peerx(d), device_id_type=MESH)
    pl.semaphore_signal(barrier, inc=1, device_id=sibling, device_id_type=MESH)

    small = [
        pltpu.make_async_copy(src, dst, ssem.at[i])
        for i, (src, dst) in enumerate(
            (
                (tok_in, tok),
                (gain1_in, gain1),
                (ids_in, ids),
                (wts_in, wts),
                (gain2_in, gain2),
            )
        )
    ]
    for load in small:
        load.start()
    loads = [
        pltpu.make_async_copy(src, dst, wsem.at[i])
        for i, (src, dst) in enumerate(
            (
                (gate.at[pl.ds(0, 128), :], w1.at[pl.ds(0, 128), pl.ds(0, DL)]),
                (up.at[pl.ds(0, 128), :], w1.at[pl.ds(128, 128), pl.ds(0, DL)]),
                (gate.at[pl.ds(128, 16), :], w1.at[pl.ds(256, 16), pl.ds(0, DL)]),
                (up.at[pl.ds(128, 16), :], w1.at[pl.ds(320, 16), pl.ds(0, DL)]),
                (down, w2.at[pl.ds(0, 144), :]),
                (egate, w3.at[pl.ds(0, DL), pl.ds(0, 256)]),
                (eup, w3.at[pl.ds(0, DL), pl.ds(256, 256)]),
                (edown, w4),
            )
        )
    ]
    for load in loads:
        load.start()

    row = iota((16, KC), 0)
    lane = iota((16, KC), 1)
    odd = lax.rem(row, 2) == 1

    def sums_of_squares(block):
        each = jnp.sum(block * block, axis=1, keepdims=True)
        each = jnp.broadcast_to(each, (16, KC))
        even_sum = jnp.sum(jnp.where(odd, 0.0, each), axis=0, keepdims=True)
        odd_sum = jnp.sum(jnp.where(odd, each, 0.0), axis=0, keepdims=True)
        total = jnp.where(odd, odd_sum, even_sum)
        high = rounded(total)
        middle = rounded(total - high)
        low = total - high - middle
        return jnp.where(
            lane == 32, high, jnp.where(lane == 33, middle, jnp.where(lane == 34, low, 0.0))
        )

    def fill_gain(layer, gain):
        gb[layer] = jnp.zeros((16, KC), F32)
        for k in range(CHUNKS):
            gb[layer, 2 * k : 2 * k + 2, :] = jnp.broadcast_to(gain[KC * k : KC * k + KC][None, :], (2, KC))

    for load in small:
        load.wait()
    stream = tok[...].astype(F32)
    tb[...] = jnp.zeros((16, KC), F32)
    for k in range(CHUNKS):
        tb[2 * k : 2 * k + 2, :] = stream[:, KC * k : KC * k + KC]
    fill_gain(0, gain1)
    lane2 = iota((2, KC), 1)
    combine = jnp.zeros((2, KC), F32)
    chosen = ids[...]
    weights = wts[...]
    for k in range(TOP):
        combine += jnp.where(chosen[:, k : k + 1] == lax.rem(lane2, EXPERTS), weights[:, k : k + 1], 0.0)
    high = rounded(combine)
    ab[...] = jnp.zeros((16, KC), F32)
    ab[14:16, :] = jnp.where(
        lane2 < EXPERTS, high, jnp.where(lane2 < 2 * EXPERTS, combine - high, 0.0)
    )

    def gather(layer, block, side, earlier):
        place_rows = chunk_rows(a2)
        mine = gath.at[layer, 0, place_rows, :]
        gath[layer, 0, place_rows, :] = jnp.where(
            row < 2 * CHUNKS, block * gb[layer], side
        ).astype(BF16)
        if layer == 0:
            pl.semaphore_wait(barrier, 2 * (N - 1) + NX)
        first = [
            send(mine, mine, ag1_s.at[layer, d], ag1_r.at[layer, d], peer2(d)) for d in FAR
        ]
        for copy in first:
            copy.start()
        line = gath.at[layer, 0]
        second = {
            d: send(line, gath.at[layer, d], ag2_s.at[layer, d], ag2_r.at[layer, d], peer1(d))
            for d in FAR
        }

        def pass_on(rows, offsets):
            for d in offsets:
                send(
                    gath.at[layer, 0, rows, :],
                    gath.at[layer, d, rows, :],
                    ag2_s.at[layer, d],
                    ag2_r.at[layer, d],
                    peer1(d),
                ).start()

        pass_on(place_rows, FIRST + LATER)
        if layer == 0:
            fill()
        else:
            for copy in earlier:
                copy.wait_send()
        held = []
        for i, copy in enumerate(reversed(first)):
            copy.wait_recv()
            rows = chunk_rows(lax.rem(a2 + N - FAR[N - 2 - i], N))
            pass_on(rows, FIRST)
            if i + 1 < EARLY:
                pass_on(rows, LATER)
            else:
                held.append(rows)
        for rows in held:
            pass_on(rows, LATER)
        forwards = {0: forward(layer, 0)}
        return first, second, forwards

    def forward(layer, d):
        copy = send(
            gath.at[layer, d],
            gath.at[layer, N + d],
            fw_s.at[layer, d],
            fw_r.at[layer, d],
            sibling,
        )
        copy.start()
        return copy

    def permuted(layer, batch, other):
        groups = [gath[layer, N * other + d] for d in BATCHES[batch]]
        moved = jnp.dot(
            perm[...], jnp.concatenate(groups, axis=1), preferred_element_type=F32
        ).astype(BF16)
        for q in range(len(groups)):
            start = 32 * START[batch] + 16 * len(groups) * other + 16 * q
            for k in range(CHUNKS + 1):
                xm[start : start + 16, KC * k : KC * k + KC] = moved[
                    16 * k : 16 * k + 16, KC * q : KC * q + KC
                ]

    def receive(layer, batch, second, forwards):
        for d in BATCHES[batch]:
            if d:
                second[d].wait_recv()
                forwards[d] = forward(layer, d)
        permuted(layer, batch, 0)
        for d in BATCHES[batch]:
            forwards[d].wait_recv()
        permuted(layer, batch, 1)

    def part_rows(batch, index):
        return pl.ds(
            pl.multiple_of(32 * START[batch] + index * XR[batch], XR[batch]), XR[batch]
        )

    def batch_rows(batch):
        return pl.ds(32 * START[batch], 32 * len(BATCHES[batch]))

    def project(layer, batch, px, rx, weight):
        rows = batch_rows(batch)
        px[rows, :] = lax.dot_general(
            xm[rows, :],
            weight[...],
            (((1,), (1 - layer,)), ((), ())),
            preferred_element_type=F32,
        ).astype(BF16)
        copies = [
            send(
                px.at[part_rows(batch, lax.rem(x + d, NX)), :],
                rx.at[d, pl.ds(8 * START[batch], XR[batch]), :],
                rx_s.at[layer, batch, d],
                rx_r.at[layer, batch, d],
                peerx(d),
            )
            for d in (2, 1, 3)
        ]
        for copy in copies:
            copy.start()
        if layer == 0:
            cw[rows, :] = jnp.dot(xm[rows, DL:], selector, preferred_element_type=F32)
        return copies

    def activate(layer, batch, px, rx, copies):
        rows = part_rows(batch, x)
        total = px[rows, :].astype(F32)
        for copy, d in zip(copies, (2, 1, 3)):
            copy.wait_recv()
            total = total + rx[d, pl.ds(8 * START[batch], XR[batch]), :].astype(F32)
        tail = total[:, total.shape[1] - 128 :]
        spot = iota((XR[batch], 128), 1)
        if layer == 0:
            used = (spot >= 96) & (spot < 99)
        else:
            used = spot < 3
        squares = jnp.sum(jnp.where(used, tail, 0.0), axis=1, keepdims=True)
        scale = lax.rsqrt(squares / D + 1e-06)
        if layer == 0:
            main = jax.nn.silu(total[:, :128] * scale) * (total[:, 128:256] * scale)
            last = jax.nn.silu(tail * scale) * (pltpu.roll(tail, 64, 1) * scale)
            last = jnp.where(spot < 16, last, 0.0)
            value = jnp.concatenate((main, last), axis=1)
        else:
            value = jax.nn.silu(total[:, :256] * scale) * (total[:, 256:512] * scale)
            share = cw[rows, :]
            value = value * jnp.concatenate((share, share), axis=1)
        hid[layer, rows, :] = value.astype(BF16)
        mine = hid.at[layer, rows, :]
        out_copies = [
            send(
                mine,
                mine,
                hx_s.at[layer, batch, d],
                hx_r.at[layer, batch, d],
                peerx(d),
            )
            for d in (2, 1, 3)
        ]
        for copy in out_copies:
            copy.start()
        return out_copies

    def lower(layer, batch, weight, copies):
        for copy in copies:
            copy.wait_recv()
        value = hid[layer, batch_rows(batch), :]
        count = 16 * len(BATCHES[batch])
        rows = pl.ds(16 * START[batch], count)
        for k in range(CHUNKS):
            part = jnp.dot(
                value[count:, :], weight[:, KC * k : KC * k + KC], preferred_element_type=F32
            )
            cs[layer, rows, KC * k : KC * k + KC] = part.astype(BF16)
        cross = []
        for q, d in enumerate(BATCHES[batch]):
            part_of = pl.ds(16 * START[batch] + 16 * q, 16)
            cross.append(
                send(
                    cs.at[layer, part_of, :],
                    cr.at[layer, part_of, :],
                    co_s.at[layer, d],
                    co_r.at[layer, d],
                    sibling,
                )
            )
            cross[q].start()
        for k in range(CHUNKS):
            of[rows, KC * k : KC * k + KC] = jnp.dot(
                value[:count, :], weight[:, KC * k : KC * k + KC], preferred_element_type=F32
            )
        return cross

    def chunk_rows(index):
        return pl.ds(pl.multiple_of(index * 16, 16), 16)

    def scatter(layer, batch, cross):
        sent = {}
        for q, d in enumerate(BATCHES[batch]):
            rows = pl.ds(16 * START[batch] + 16 * q, 16)
            cross[q].wait_recv()
            value = of[rows, :] + cr[layer, rows, :].astype(F32)
            s1[layer, rows, :] = value.astype(BF16)
            if d:
                sent[d] = send(
                    s1.at[layer, rows, :],
                    r1.at[layer, d],
                    r1_s.at[layer, d],
                    r1_r.at[layer, d],
                    peer1(N - d),
                )
                sent[d].start()
            else:
                r1[layer, 0] = value.astype(BF16)
        return sent

    def collect(layer, first, started):
        total = r1[layer, 0].astype(F32)
        for d in FAR:
            first[d].wait_recv()
            total = total + r1[layer, d].astype(F32)
        total = total.astype(BF16)
        stacked = jnp.concatenate(
            [total[:, KC * k : KC * k + KC] for k in range(CHUNKS)] + [jnp.zeros((16, KC), BF16)],
            axis=0,
        )
        s2[layer] = jnp.dot(perm[...], stacked, preferred_element_type=F32).astype(BF16)
        second = {}
        for d in FAR:
            second[d] = send(
                s2.at[layer, chunk_rows(lax.rem(a2 + d, N)), :],
                r2.at[layer, d],
                r2_s.at[layer, d],
                r2_r.at[layer, d],
                peer2(d),
            )
            second[d].start()
        for copy in started:
            copy.wait_send()
        total = s2[layer, chunk_rows(a2), :].astype(F32)
        for d in NEAR:
            second[d].wait_recv()
            total = total + r2[layer, d].astype(F32)
        return total, list(second.values())

    def layer_of(layer, block, side, px, rx, w_in, w_out, loads_in, loads_out, earlier):
        first, second, forwards = gather(layer, block, side, earlier)
        parts, hiddens, crossed, sent = {}, {}, {}, {}
        for step in STEPS:
            b = int(step[1])
            if step == "r0":
                receive(layer, b, second, forwards)
                for load in loads_in:
                    load.wait()
                parts[b] = project(layer, b, px, rx, w_in)
            elif step[0] == "r":
                receive(layer, b, second, forwards)
                parts[b] = project(layer, b, px, rx, w_in)
            elif step[0] == "a":
                hiddens[b] = activate(layer, b, px, rx, parts[b])
            elif step[0] == "l":
                if b == 0:
                    for load in loads_out:
                        load.wait()
                crossed[b] = lower(layer, b, w_out, hiddens[b])
            else:
                sent.update(scatter(layer, b, crossed[b]))
        started = list(first)
        for group in (parts, hiddens, crossed):
            started += [copy for copies in group.values() for copy in copies]
        for group in (second, forwards, sent):
            started += group.values()
        return collect(layer, sent, started)

    expert = dp // (EH // 256)
    at = iota((KC, 128), 0)
    selector = ((at == expert) | (at == expert + EXPERTS)).astype(F32).astype(BF16)

    def fill():
        fill_gain(1, gain2)
        to = iota((128, 128), 0)
        source = lax.rem(to // 2, 8) * 16 + (to // 16) * 2 + lax.rem(to, 2)
        perm[...] = (source == iota((128, 128), 1)).astype(F32).astype(BF16)
        side_row = iota((KC, 128), 0)
        side_lane = iota((KC, 128), 1)
        is_part = (side_row >= 32) & (side_row < 35)
        w1[:256, DL:] = jnp.zeros((256, KC), BF16)
        w1[272:320, :DL] = jnp.zeros((48, DL), BF16)
        w1[336:, :DL] = jnp.zeros((48, DL), BF16)
        to_row = iota((128, KC), 0)
        to_lane = iota((128, KC), 1)
        wanted = (to_lane >= 32) & (to_lane < 35) & (to_row == to_lane + 64)
        w1[256:, DL:] = wanted.astype(F32).astype(BF16)
        w2[144:, :] = jnp.zeros((112, DL), BF16)
        w3[DL:, :512] = jnp.zeros((KC, 512), BF16)
        w3[:DL, 512:] = jnp.zeros((DL, 128), BF16)
        w3[DL:, 512:] = (is_part & (side_lane == side_row - 32)).astype(F32).astype(BF16)

    tokens_block = tb[...]
    side = jnp.where(row >= 14, ab[...] + sums_of_squares(tokens_block), 0.0)
    dense, pending = layer_of(
        0, tokens_block, side, px0, rx0, w1, w2, loads[0:4], loads[4:5], ()
    )
    mixed = rounded(tb[...] + dense)
    mixed = jnp.where(row < 2 * CHUNKS, mixed, 0.0)
    tb[...] = mixed
    side = jnp.where(row >= 14, sums_of_squares(mixed), 0.0)
    routed, more = layer_of(
        1, mixed, side, px1, rx1, w3, w4, loads[5:7], loads[7:], pending
    )
    tb[...] = tb[...] + routed
    live = iota((2, KC), 0) < newt[0]
    for k in range(CHUNKS):
        out[:, KC * k : KC * k + KC] = jnp.where(live, tb[2 * k : 2 * k + 2, :], 0.0)
    for copy in more:
        copy.wait_send()


def shards(
    tokens,
    new_tokens,
    dense_gain,
    dense_gate,
    dense_up,
    dense_down,
    moe_gain,
    expert_ids,
    expert_weights,
    expert_gate,
    expert_up,
    expert_down,
):
    vmem = pl.BlockSpec(memory_space=pltpu.VMEM)
    smem = pl.BlockSpec(memory_space=pltpu.SMEM)
    anywhere = pl.BlockSpec(memory_space=pltpu.HBM)
    sems = pltpu.SemaphoreType.DMA
    result = pl.pallas_call(
        kernel,
        out_shape=jax.ShapeDtypeStruct((2, DL), F32),
        in_specs=[anywhere, smem] + [anywhere] * 10,
        out_specs=vmem,
        scratch_shapes=[
            pltpu.VMEM((2, DL), BF16),
            pltpu.VMEM((DL,), F32),
            pltpu.VMEM((DL,), F32),
            pltpu.VMEM((2, TOP), jnp.int32),
            pltpu.VMEM((2, TOP), F32),
            pltpu.VMEM((384, DL + KC), BF16),
            pltpu.VMEM((256, DL), BF16),
            pltpu.VMEM((DL + KC, 640), BF16),
            pltpu.VMEM((256, DL), BF16),
            pltpu.VMEM((16, KC), F32),
            pltpu.VMEM((2, 16, KC), F32),
            pltpu.VMEM((16, KC), F32),
            pltpu.VMEM((128, 128), BF16),
            pltpu.VMEM((2, 2 * N, 128, KC), BF16),
            pltpu.VMEM((2 * HALF, DL + KC), BF16),
            pltpu.VMEM((2 * HALF, 128), F32),
            pltpu.VMEM((2 * HALF, 384), BF16),
            pltpu.VMEM((2 * HALF, 640), BF16),
            pltpu.VMEM((NX, 64, 384), BF16),
            pltpu.VMEM((NX, 64, 640), BF16),
            pltpu.VMEM((2, 2 * HALF, 256), BF16),
            pltpu.VMEM((2, HALF, DL), BF16),
            pltpu.VMEM((2, HALF, DL), BF16),
            pltpu.VMEM((HALF, DL), F32),
            pltpu.VMEM((2, HALF, DL), BF16),
            pltpu.VMEM((2, N, 16, DL), BF16),
            pltpu.VMEM((2, 128, KC), BF16),
            pltpu.VMEM((2, N, 16, KC), BF16),
            sems((5,)),
            sems((8,)),
            sems((2, N)),
            sems((2, N)),
            sems((2, N)),
            sems((2, N)),
            sems((2, N)),
            sems((2, N)),
            sems((2, len(BATCHES), NX)),
            sems((2, len(BATCHES), NX)),
            sems((2, len(BATCHES), NX)),
            sems((2, len(BATCHES), NX)),
            sems((2, N)),
            sems((2, N)),
            sems((2, N)),
            sems((2, N)),
            sems((2, N)),
            sems((2, N)),
        ],
        compiler_params=pltpu.CompilerParams(
            collective_id=0, has_side_effects=True, vmem_limit_bytes=60 * 1024 * 1024
        ),
        name="layers",
    )(
        tokens,
        new_tokens,
        dense_gain,
        dense_gate.T,
        dense_up.T,
        dense_down,
        moe_gain,
        expert_ids,
        expert_weights,
        expert_gate,
        expert_up,
        expert_down,
    )
    return result.astype(BF16)


def solution(mesh):
    placed = (
        P("dp", "sub"),
        P("dp"),
        P("sub"),
        P("sub", "dp"),
        P("sub", "dp"),
        P("dp", "sub"),
        P("sub"),
        P("dp", None),
        P("dp", None),
        P("sub", "dp"),
        P("sub", "dp"),
        P("dp", "sub"),
    )
    return jax.shard_map(
        shards, mesh=mesh, in_specs=placed, out_specs=P("dp", "sub"), check_vma=False
    )
```
